128 devices in a mesh: aux: 32 (over y, z, core), grp: 4 (over x).
Axes of the slice: x: 4, y: 4, z: 4, core: 2. Of those that a mesh axis runs over, the one named last changes fastest.
Arguments:
- ao_blocks: bfloat16 [1024, 32, 32, 384], P(('aux', 'grp')), may hold values from -6 to 6
- blocks: int32 [1024, 4], P(('aux', 'grp')), may hold values from 0 to 12288, as said below
- occ_coeff: bfloat16 [2, 4352], replicated, may hold values from -0.75 to 0.75
- vir_coeff: bfloat16 [4352, 4096], P('grp'), may hold values from -0.09375 to 0.09375
- occ_energy: float32 [2], replicated, may hold values from -1.5 to -0.3
- vir_energy: float32 [4096], replicated, may hold values from 0.1 to 6
- owner: int32 [128], replicated, may hold values from 0 to 127, each once
Outputs:
- density_half: bfloat16 [2, 4352, 12288], P(None, 'grp', 'aux')
The draws below stay inside these ranges and needn't reach their ends.
Inputs may be any that keep to these rules, and one draw needn't show every extreme that they name: `blocks`: row k belongs to device k // 8 in mesh order (aux slowest): its nu shell block lies in that device's AO quarter (q * 34 to (q + 1) * 34 - 1), its range lo <= hi lies inside that device's aux slice s * 384 to (s + 1) * 384; slots with lo == hi are empty and follow the live ones; every device has 1 to 8 live slots, its first one covers the whole slice, and some device has 8. `owner`: each device index once.
All inputs are finite; a program needn't handle non-finite values.
Results may differ from the reference program's by a relative error of at most 0.015.
Values may be sent and summed in bfloat16 or wider, within the bound.
No kernel may reach another device: no remote copies, remote signals or barrier semaphores. Data moves between devices by JAX's collectives and lax.ppermute only.
A program may use at most 128 MiB of HBM per device.

```python
import math
import jax
import jax.numpy as jnp
from jax import lax

NVIR = 4096
NAUX = 12288
NAO = 4352
SB = 32
OI = 2
NB = 8
AUXD = 384
NAOQ = 1088
NSH = 136
OVB = 64
NBLK = 1024
N_AUX = 32
N_GRP = 4
DEVICES = 128


def draw_blocks(key, part):
    key = jax.random.fold_in(key, 11)
    keys = jax.random.split(key, 5)
    slots = jnp.arange(NBLK, dtype=jnp.int32)
    device = slots // NB
    local = slots % NB
    slice_id = device // N_GRP
    quarter = device % N_GRP
    quarter_shells = NAOQ // SB
    mu_block = jax.random.randint(keys[0], (NBLK,), 0, NSH, dtype=jnp.int32)
    nu_block = quarter * quarter_shells + jax.random.randint(keys[1], (NBLK,), 0, quarter_shells, dtype=jnp.int32)
    start = slice_id * AUXD
    lower = start + jax.random.randint(keys[2], (NBLK,), 0, AUXD // 2, dtype=jnp.int32)
    upper = start + AUXD - jax.random.randint(keys[3], (NBLK,), 0, AUXD // 2, dtype=jnp.int32)
    lower = jnp.where(local == 0, start, lower)
    upper = jnp.where(local == 0, start + AUXD, upper)
    live_count = jax.random.randint(keys[4], (DEVICES,), 1, NB + 1, dtype=jnp.int32)
    live_count = live_count.at[0].set(NB)
    alive = local < jnp.take(live_count, device)
    lower = jnp.where(alive, lower, start)
    upper = jnp.where(alive, upper, start)
    return jnp.stack([mu_block, nu_block, lower, upper], axis=1).astype(jnp.int32)


def steps_of(key, shape, shards, least, top_value):
    gain = 1.0
    for axis_at, blocks in shards:
        steps = jax.random.uniform(jax.random.fold_in(jax.random.fold_in(key, 6), axis_at), (blocks,), jnp.float32, least / len(shards), top_value / len(shards))
        gain = gain * jnp.repeat(jnp.exp(steps), shape[axis_at] // blocks).reshape((-1,) + (1,) * (len(shape) - 1 - axis_at))
    return gain


def scatter_about(key, extent, scale, reach, shards=(), kind=jnp.bfloat16):
    entries = scale * jax.random.normal(key, extent, jnp.float32)
    if shards:
        entries = entries * steps_of(key, extent, shards, -0.22, 0.18)
    return jnp.clip(entries, -reach, reach).astype(kind)


def setup_inputs(seed: int = 0) -> dict:
    key_list = jax.random.split(jax.random.key(seed), 8)
    ao_blocks = scatter_about(key_list[0], (NBLK, SB, SB, AUXD), 1.0, 6.0, ((0, 128),))
    blocks = draw_blocks(jax.random.fold_in(key_list[7], 71), 0)
    occ_coeff = scatter_about(key_list[2], (OI, NAO), 0.05, 0.75)
    vir_coeff = scatter_about(key_list[3], (NAO, NVIR), NVIR ** -0.5, 0.09375, ((0, 4),))
    occ_energy = jnp.clip(jax.random.uniform(key_list[4], (OI,), jnp.float32, -1.5, -0.3), -1.5, -0.3)
    vir_energy = jnp.clip(jnp.exp(jax.random.uniform(key_list[5], (NVIR,), jnp.float32, math.log(0.1), math.log(6.0))), 0.1, 6.0)
    owner = jax.random.permutation(key_list[6], DEVICES).astype(jnp.int32)
    return dict(ao_blocks=ao_blocks, blocks=blocks, occ_coeff=occ_coeff, vir_coeff=vir_coeff, occ_energy=occ_energy, vir_energy=vir_energy, owner=owner)


def block_term(ao_tile, occ_rows, vir_rows, lower, upper, first):
    half_tile = jnp.einsum('im,mnp->inp', occ_rows.astype(jnp.float32), ao_tile.astype(jnp.float32))
    positions = first + jnp.arange(ao_tile.shape[2], dtype=jnp.int32)
    inside = ((positions >= lower) & (positions < upper)).astype(jnp.float32)
    half_tile = (half_tile * inside).astype(jnp.bfloat16)
    return jnp.einsum('na,inp->iap', vir_rows.astype(jnp.float32), half_tile.astype(jnp.float32))


def reference(ao_blocks, blocks, occ_coeff, vir_coeff, occ_energy, vir_energy, owner):
    def slice_rows(slice_id):
        first = (slice_id * AUXD).astype(jnp.int32)

        def one_quarter(quarter):
            base = ((slice_id * N_GRP + quarter) * NB).astype(jnp.int32)

            def add_block(step, total):
                where = (base + step).astype(jnp.int32)
                entry = lax.dynamic_index_in_dim(blocks, where, 0, keepdims=False)
                ao_tile = lax.dynamic_index_in_dim(ao_blocks, where, 0, keepdims=False)
                occ_rows = lax.dynamic_slice_in_dim(occ_coeff, (entry[0] * SB).astype(jnp.int32), SB, 1)
                vir_rows = lax.dynamic_slice_in_dim(vir_coeff, (entry[1] * SB).astype(jnp.int32), SB, 0)
                return total + block_term(ao_tile, occ_rows, vir_rows, entry[2], entry[3], first)

            partial_value = lax.fori_loop(0, NB, add_block, jnp.zeros((OI, NVIR, AUXD), jnp.float32))
            return partial_value.astype(jnp.bfloat16)

        partials = lax.map(one_quarter, jnp.arange(N_GRP, dtype=jnp.int32))
        return jnp.sum(partials.astype(jnp.float32), axis=0).astype(jnp.bfloat16)

    slices = lax.map(slice_rows, jnp.arange(N_AUX, dtype=jnp.int32))
    coeffs = jnp.transpose(slices, (1, 2, 0, 3)).reshape(OI * NVIR, NAUX)
    pair_energy = (occ_energy[:, None] - vir_energy[None, :]).reshape(OI * NVIR)
    slot_block = jnp.zeros((DEVICES,), jnp.int32).at[owner].set(jnp.arange(DEVICES, dtype=jnp.int32))
    coeff_blocks = coeffs.reshape(DEVICES, OVB, NAUX)
    energy_blocks = pair_energy.reshape(DEVICES, OVB)

    def group_density(group):
        members = lax.dynamic_slice_in_dim(slot_block, (group * N_GRP).astype(jnp.int32), N_GRP)
        panel = jnp.take(coeff_blocks, members, axis=0).reshape(N_GRP * OVB, NAUX)
        panel_energy = jnp.take(energy_blocks, members, axis=0).reshape(N_GRP * OVB)
        scores = jnp.dot(panel, panel.T, preferred_element_type=jnp.float32)
        amplitude = (scores / (panel_energy[:, None] + panel_energy[None, :])).astype(jnp.bfloat16)
        return jnp.dot(amplitude, panel, preferred_element_type=jnp.float32).astype(jnp.bfloat16)

    grouped = lax.map(group_density, jnp.arange(N_AUX, dtype=jnp.int32))
    density = jnp.take(grouped.reshape(DEVICES, OVB, NAUX), owner, axis=0).reshape(OI, NVIR, NAUX)

    def back_slice(slice_id):
        piece = lax.dynamic_slice_in_dim(density, (slice_id * AUXD).astype(jnp.int32), AUXD, 2)
        result = jnp.einsum('na,iap->inp', vir_coeff.astype(jnp.float32), piece.astype(jnp.float32))
        return result.astype(jnp.bfloat16)

    halves = lax.map(back_slice, jnp.arange(N_AUX, dtype=jnp.int32))
    return jnp.transpose(halves, (1, 2, 0, 3)).reshape(OI, NAO, NAUX)
```

```python
import functools

import jax
import jax.numpy as jnp
from jax import lax
from jax.experimental import pallas as pl
from jax.experimental.pallas import tpu as pltpu
from jax.sharding import PartitionSpec as P

BF = jnp.bfloat16
F32 = jnp.float32
CHUNKS = 2
STEP_GROUPS = 4


def pair_of_blocks(left, right, left_odd, right_odd, lane):
    def swapped(tile):
        return jnp.concatenate([tile[:, 64:], tile[:, :64]], axis=1)

    low = jnp.where(left_odd == 1, swapped(left), left)
    high = jnp.where(right_odd == 1, right, swapped(right))
    return jnp.where(lane < 64, low, high)


def partial_kernel(
    blocks, owner, place, occ, ao, *refs, slots, groups, width, shell, grp_count, chunk_rows
):
    vir = refs[:slots]
    outs = refs[slots:-4]
    half, half_abs, half_rel, slot_block = refs[-4:]
    step = pl.program_id(0)
    slice_rows = width // grp_count
    blocks_per_occ = owner.shape[0] // 2

    @pl.when(step == 0)
    def _():
        def put(b, carry):
            slot_block[owner[b]] = b
            return carry

        lax.fori_loop(0, owner.shape[0], put, 0)

    @pl.when(step < slots)
    def _():
        base = blocks[step, 0] * shell
        totals = [jnp.zeros((shell, width), F32) for _ in range(2)]
        for mu in range(shell):
            tile = ao[0, mu].astype(F32)
            for i in range(2):
                totals[i] = totals[i] + occ[i, base + mu] * tile
        position = lax.broadcasted_iota(jnp.int32, (shell, width), 1) + place[0] * width
        inside = (position >= blocks[step, 2]) & (position < blocks[step, 3])
        for i in range(2):
            rows = pl.ds(pl.multiple_of(step * shell, shell), shell)
            half[i, rows, :] = jnp.where(inside, totals[i], 0.0).astype(BF)

    @pl.when(step == slots)
    def _():
        for i in range(2):
            half_abs[i] = half[i].T
        for i in range(2):
            for r in range(grp_count):
                source = lax.rem(place[1] + r, grp_count) * slice_rows
                half_rel[i, pl.ds(r * slice_rows, slice_rows), :] = half_abs[
                    i, pl.ds(pl.multiple_of(source, 16), slice_rows), :
                ]

    @pl.when(step >= slots)
    def _():
        turn = step - slots
        first_half = turn < groups // STEP_GROUPS // 2
        lane = lax.broadcasted_iota(jnp.int32, (slots * shell, 128), 1)
        wide_lane = lax.broadcasted_iota(jnp.int32, (width, 256), 1)
        for at in range(STEP_GROUPS):
            g = turn * STEP_GROUPS + at
            tiles = []
            occ_is = []
            for pair in range(2):
                found = [slot_block[g * 4 + pair * 2 + j] for j in range(2)]
                read = []
                for b in found:
                    column = lax.rem(b, blocks_per_occ)
                    occ_is.append(b // blocks_per_occ)
                    lanes = pl.ds(pl.multiple_of((column // 2) * 128, 128), 128)
                    read.append(jnp.concatenate([v[:, lanes] for v in vir], axis=0))
                odd = [lax.rem(b, 2) for b in found]
                tiles.append(pair_of_blocks(read[0], read[1], odd[0], odd[1], lane))
            panel = jnp.concatenate(tiles, axis=1)
            both = [jnp.dot(half_rel[i], panel, preferred_element_type=F32) for i in range(2)]
            which = jnp.where(
                wide_lane < 128,
                jnp.where(wide_lane < 64, occ_is[0], occ_is[1]),
                jnp.where(wide_lane < 192, occ_is[2], occ_is[3]),
            )
            value = jnp.where(which == 0, both[0], both[1]).astype(BF)
            for c in range(CHUNKS):

                def rows(r):
                    begin = r * slice_rows + c * chunk_rows
                    return value[begin : begin + chunk_rows]

                mine = outs[c * 7 : c * 7 + 7]
                mine[0][at] = rows(0)

                @pl.when(first_half)
                def _():
                    mine[1][at] = rows(1)
                    mine[2][at] = rows(2)
                    mine[3][at] = rows(3)

                @pl.when(jnp.logical_not(first_half))
                def _():
                    mine[4][at] = rows(1)
                    mine[5][at] = rows(2)
                    mine[6][at] = rows(3)


def partial_pieces(ao_blocks, blocks, occ, vir_coeff, owner, place, groups):
    slots, shell, _, width = ao_blocks.shape
    virtuals = vir_coeff.shape[1]
    grp_count = 4
    chunk_rows = width // grp_count // CHUNKS
    turns = groups // STEP_GROUPS
    half_turns = turns // 2

    def vir_spec(k):
        return pl.BlockSpec((shell, virtuals), lambda t, blk, own, plc, oc: (blk[k, 1], 0))

    whole = pl.BlockSpec(
        (STEP_GROUPS, chunk_rows, 256), lambda t, *_: (jnp.maximum(t - slots, 0), 0, 0)
    )
    early = pl.BlockSpec(
        (STEP_GROUPS, chunk_rows, 256),
        lambda t, *_: (jnp.clip(t - slots, 0, half_turns - 1), 0, 0),
    )
    late = pl.BlockSpec(
        (STEP_GROUPS, chunk_rows, 256),
        lambda t, *_: (jnp.maximum(t - slots - half_turns, 0), 0, 0),
    )
    out_specs = ([whole] + [early] * 3 + [late] * 3) * CHUNKS
    full = jax.ShapeDtypeStruct((groups, chunk_rows, 256), BF)
    part = jax.ShapeDtypeStruct((groups // 2, chunk_rows, 256), BF)
    out_shape = ([full] + [part] * 6) * CHUNKS
    kernel = functools.partial(
        partial_kernel,
        slots=slots,
        groups=groups,
        width=width,
        shell=shell,
        grp_count=grp_count,
        chunk_rows=chunk_rows,
    )
    return pl.pallas_call(
        kernel,
        grid_spec=pltpu.PrefetchScalarGridSpec(
            num_scalar_prefetch=4,
            grid=(slots + turns,),
            in_specs=[
                pl.BlockSpec(
                    (1, shell, shell, width),
                    lambda t, *_: (jnp.minimum(t, slots - 1), 0, 0, 0),
                )
            ]
            + [vir_spec(k) for k in range(slots)],
            out_specs=out_specs,
            scratch_shapes=[
                pltpu.VMEM((2, slots * shell, width), BF),
                pltpu.VMEM((2, width, slots * shell), BF),
                pltpu.VMEM((2, width, slots * shell), BF),
                pltpu.SMEM((owner.shape[0],), jnp.int32),
            ],
        ),
        out_shape=out_shape,
        compiler_params=pltpu.CompilerParams(vmem_limit_bytes=48 * 1024 * 1024),
        cost_estimate=pl.CostEstimate(
            flops=4 * 1024 * 1024 * 1024, bytes_accessed=16 * 1024 * 1024, transcendentals=0
        ),
        name="partial_rows",
    )(blocks, owner, place, occ, ao_blocks, *([vir_coeff] * slots))


def back_kernel(owner, place, vir, *refs, groups, width, grp_count, chunk_rows):
    pieces = refs[: CHUNKS * 8]
    out = refs[CHUNKS * 8]
    density = refs[-1]
    slice_rows = width // grp_count
    half_groups = groups // 2
    tiles = density.shape[2] // 128

    @pl.when(pl.program_id(0) == 0)
    def _():
        lane = lax.broadcasted_iota(jnp.int32, (chunk_rows, 128), 1)

        def tile_of(t, carry):
            for i in range(2):
                slots = [owner[i * 2 * tiles + t * 2 + j] for j in range(2)]
                low_group = [d // 4 for d in slots]
                tile_at = [lax.rem(d // 2, 2) * 128 for d in slots]
                odd = [lax.rem(d, 2) for d in slots]
                for c in range(CHUNKS):
                    for r in range(grp_count):
                        pair = pieces[c * 8 + r * 2 : c * 8 + r * 2 + 2]
                        read = []
                        for j in range(2):
                            lanes = pl.ds(pl.multiple_of(tile_at[j], 128), 128)
                            inside = lax.rem(low_group[j], half_groups)
                            read.append(
                                jnp.where(
                                    low_group[j] < half_groups,
                                    pair[0][inside, :, lanes],
                                    pair[1][inside, :, lanes],
                                )
                            )
                        source = lax.rem(place[1] + r, grp_count) * slice_rows + c * chunk_rows
                        density[
                            i,
                            pl.ds(pl.multiple_of(source, 16), chunk_rows),
                            pl.ds(pl.multiple_of(t * 128, 128), 128),
                        ] = pair_of_blocks(read[0], read[1], odd[0], odd[1], lane)
            return carry

        lax.fori_loop(0, tiles, tile_of, 0)

    for i in range(2):
        out[i] = lax.dot_general(
            vir[...], density[i], (((1,), (1,)), ((), ())), preferred_element_type=F32
        ).astype(BF)


def back_transform(vir_coeff, owner, place, pieces, groups, width):
    rows, virtuals = vir_coeff.shape
    grp_count = 4
    chunk_rows = width // grp_count // CHUNKS
    tile_rows = 272
    piece = pl.BlockSpec((groups // 2, chunk_rows, 256), lambda t, *_: (0, 0, 0))
    return pl.pallas_call(
        functools.partial(
            back_kernel, groups=groups, width=width, grp_count=grp_count, chunk_rows=chunk_rows
        ),
        grid_spec=pltpu.PrefetchScalarGridSpec(
            num_scalar_prefetch=2,
            grid=(rows // tile_rows,),
            in_specs=[pl.BlockSpec((tile_rows, virtuals), lambda t, *_: (t, 0))]
            + [piece] * (CHUNKS * 8),
            out_specs=pl.BlockSpec((2, tile_rows, width), lambda t, *_: (0, t, 0)),
            scratch_shapes=[pltpu.VMEM((2, width, virtuals), BF)],
        ),
        out_shape=jax.ShapeDtypeStruct((2, rows, width), BF),
        compiler_params=pltpu.CompilerParams(vmem_limit_bytes=56 * 1024 * 1024),
        cost_estimate=pl.CostEstimate(
            flops=7 * 1024 * 1024 * 1024, bytes_accessed=18 * 1024 * 1024, transcendentals=0
        ),
        name="back_transform",
    )(owner, place, vir_coeff, *pieces)


def body(ao_blocks, blocks, occ_coeff, vir_coeff, occ_energy, vir_energy, owner):
    aux_place = lax.axis_index("aux")
    grp_place = lax.axis_index("grp")
    groups = lax.axis_size("aux")
    grp_count = lax.axis_size("grp")
    devices = groups * grp_count
    virtuals = vir_coeff.shape[1]
    shell = ao_blocks.shape[1]
    width = ao_blocks.shape[3]
    quarter_shells = vir_coeff.shape[0] // shell
    block_rows = 2 * virtuals // devices
    place = jnp.stack([aux_place, grp_place]).astype(jnp.int32)
    local_blocks = blocks - jnp.array([0, 1, 0, 0], jnp.int32)[None, :] * (grp_place * quarter_shells)
    pieces = partial_pieces(
        ao_blocks, local_blocks, occ_coeff.astype(F32), vir_coeff, owner, place, groups
    )

    def shift(value, by):
        return lax.ppermute(
            value, "grp", [(j, (j + by) % grp_count) for j in range(grp_count)]
        )

    device_ids = jnp.arange(devices, dtype=jnp.int32)
    members = aux_place * grp_count + jnp.arange(grp_count, dtype=jnp.int32)
    member_block = jnp.sum(
        (owner[None, :] == members[:, None]).astype(jnp.int32) * device_ids[None, :], axis=1
    )
    row_ids = (member_block[:, None] * block_rows + jnp.arange(block_rows, dtype=jnp.int32)).reshape(-1)
    pair_energy = (occ_energy[:, None] - vir_energy[None, :]).reshape(devices, block_rows)
    picked = (member_block[:, None] == device_ids[None, :]).astype(F32)
    panel_energy = jnp.sum(picked[:, :, None] * pair_energy[None], axis=1).reshape(-1)
    del row_ids

    arrived = []
    scores = None
    for c in range(CHUNKS):
        own, one_a, two_a, three_a, one_b, two_b, three_b = pieces[c * 7 : c * 7 + 7]
        relay_up = shift(two_a, 1)
        relay_down = shift(two_b, -1)
        up_b = shift(one_b, 1)
        down_a = shift(three_a, -1)
        up_a = shift((one_a.astype(F32) + relay_up.astype(F32)).astype(BF), 1)
        down_b = shift((three_b.astype(F32) + relay_down.astype(F32)).astype(BF), -1)
        half = groups // 2
        total = own.astype(F32) + jnp.concatenate(
            [
                up_a.astype(F32) + down_a.astype(F32),
                up_b.astype(F32) + down_b.astype(F32),
            ],
            axis=0,
        )
        rows = lax.all_to_all(total.astype(BF), "aux", split_axis=0, concat_axis=0, tiled=True)
        rows = rows.reshape(-1, 256)
        arrived.append(rows)
        term = lax.dot_general(rows, rows, (((0,), (0,)), ((), ())), preferred_element_type=F32)
        scores = term if scores is None else scores + term

    sent = scores.astype(BF)
    others = [shift(sent, by) for by in (1, 2, 3)]
    scores = scores + others[0].astype(F32) + others[1].astype(F32) + others[2].astype(F32)
    amplitude = (scores / (panel_energy[:, None] + panel_energy[None, :])).astype(BF)

    gathered = []
    for c in range(CHUNKS):
        density = jnp.dot(arrived[c], amplitude, preferred_element_type=F32).astype(BF)
        density = density.reshape(groups, -1, 256)
        back = lax.all_to_all(density, "aux", split_axis=0, concat_axis=0, tiled=True)
        first, second = back[: groups // 2], back[groups // 2 :]
        below_a, below_b = shift(first, 1), shift(second, 1)
        above_a, above_b = shift(first, -1), shift(second, -1)
        far_a = shift(below_a, 1)
        far_b = shift(above_b, -1)
        gathered += [first, second, above_a, above_b, far_a, far_b, below_a, below_b]

    return back_transform(vir_coeff, owner, place, gathered, groups, width)


def solution(mesh):
    return jax.shard_map(
        body,
        mesh=mesh,
        in_specs=(
            P(("aux", "grp"), None, None, None),
            P(("aux", "grp"), None),
            P(),
            P("grp", None),
            P(),
            P(),
            P(),
        ),
        out_specs=P(None, "grp", "aux"),
        check_vma=False,
    )
```

```python
import functools

import jax
import jax.numpy as jnp
from jax import lax
from jax.experimental import pallas as pl
from jax.experimental.pallas import tpu as pltpu
from jax.sharding import PartitionSpec as P

BF = jnp.bfloat16
F32 = jnp.float32
CHUNKS = 2
SLOTS_PER_STEP = 2
GRP = 4
MIB = 1024 * 1024
VMEM = pl.BlockSpec(memory_space=pltpu.VMEM)
SMEM = pl.BlockSpec(memory_space=pltpu.SMEM)


def swapped(tile):
    return jnp.concatenate([tile[:, 64:], tile[:, :64]], axis=1)


def half_at(tile, block, place):
    return jnp.where(lax.rem(block, 2) == place, tile, swapped(tile))


def invert(owner, slot_block):
    def put(b, carry):
        slot_block[owner[b]] = b
        return carry

    lax.fori_loop(0, owner.shape[0], put, 0)


def multiply(half_rows, vir, natural):
    inner = half_rows.shape[1] // 2
    tiles = natural.shape[0] // 2
    for t in range(tiles // 2):
        panel = jnp.concatenate([v[:, t * 256 : (t + 1) * 256] for v in vir], axis=0)
        for i in range(2):
            product = jnp.dot(
                half_rows[:, i * inner : (i + 1) * inner], panel, preferred_element_type=F32
            ).astype(BF)
            for j in range(2):
                natural[i * tiles + t * 2 + j] = product[:, j * 128 : (j + 1) * 128]


def owner_order(natural, slot_block, groups, store):
    lane = lax.broadcasted_iota(jnp.int32, natural.shape[1:], 1)

    def one(g):
        for pair in range(2):
            tiles = []
            for j in range(2):
                b = slot_block[g * 4 + pair * 2 + j]
                tiles.append(half_at(natural[b // 2], b, j))
            value = jnp.where(lane < 64, tiles[0], tiles[1])
            store(g, slice(pair * 128, (pair + 1) * 128), value)

    def two(t, carry):
        one(t * 2)
        one(t * 2 + 1)
        return carry

    lax.fori_loop(groups[0] // 2, groups[1] // 2, two, 0)


def far_kernel(blocks, owner, occ, ao, *refs, slots, groups, width, shell, quarter_shells):
    vir = refs[:slots]
    rest, *outs = refs[slots : slots + 1 + 2 * CHUNKS]
    half, half_abs, far_rows, natural, slot_block = refs[-5:]
    step = pl.program_id(0)
    inner = slots * shell
    rows = width // GRP // CHUNKS
    first_position = blocks[0, 2]
    quarter = blocks[0, 1] // quarter_shells

    position = lax.broadcasted_iota(jnp.int32, (shell, width), 1) + first_position
    spread = (128, shell * shell)
    source_lane = lax.broadcasted_iota(jnp.int32, spread, 0)
    target_mu = lax.broadcasted_iota(jnp.int32, spread, 1) // shell
    row = lax.broadcasted_iota(jnp.int32, (shell, shell * shell), 0)
    column = lax.broadcasted_iota(jnp.int32, (shell, shell * shell), 1)
    diagonal = lax.rem(column, shell) == row
    per_tile = 128 // shell
    for s in range(SLOTS_PER_STEP):
        k = step * SLOTS_PER_STEP + s
        inside = (position >= blocks[k, 2]) & (position < blocks[k, 3])
        mu_block = blocks[k, 0]
        lanes = pl.ds(pl.multiple_of((mu_block // per_tile) * 128, 128), 128)
        pick = source_lane == target_mu + lax.rem(mu_block, per_tile) * shell
        wide = jnp.dot(
            occ[:, lanes], jnp.where(pick, 1.0, 0.0).astype(BF), preferred_element_type=F32
        )
        weights = jnp.concatenate(
            [
                jnp.where(
                    diagonal, jnp.broadcast_to(wide[i : i + 1, :], (shell, shell * shell)), 0.0
                )
                for i in range(2)
            ],
            axis=0,
        ).astype(BF)
        both = jnp.dot(
            weights, ao[s].reshape(shell * shell, width), preferred_element_type=F32
        )
        for i in range(2):
            at = pl.ds(pl.multiple_of(k * shell, shell), shell)
            half[i, at, :] = jnp.where(inside, both[i * shell : (i + 1) * shell], 0.0).astype(BF)

    @pl.when(step == 0)
    def _():
        invert(owner, slot_block)

    @pl.when(step == slots // SLOTS_PER_STEP - 1)
    def _():
        for i in range(2):
            half_abs[:, i * inner : (i + 1) * inner] = half[i].T
        for at, r in enumerate((2, 0, 1, 3)):
            for c in range(CHUNKS):
                source = (c * GRP + lax.rem(quarter + r, GRP)) * rows
                value = half_abs[pl.ds(pl.multiple_of(source, 16), rows), :]
                if r == 2:
                    far_rows[c * rows : (c + 1) * rows, :] = value
                else:
                    begin = ((at - 1) * CHUNKS + c) * rows
                    rest[begin : begin + rows, :] = value
        multiply(far_rows, vir, natural)
        for h in range(2):

            def store(g, lanes, value):
                for c in range(CHUNKS):
                    outs[c * 2 + h][g - h * (groups // 2), :, lanes] = value[
                        c * rows : (c + 1) * rows
                    ]

            owner_order(
                natural, slot_block, (h * (groups // 2), (h + 1) * (groups // 2)), store
            )


def near_kernel(blocks, owner, half_rows, *refs, slots, groups):
    vir = refs[:slots]
    outs = refs[slots : slots + 5 * CHUNKS]
    natural, slot_block = refs[-2:]
    rows = half_rows.shape[0] // (3 * CHUNKS)
    half = groups // 2
    invert(owner, slot_block)
    multiply(half_rows, vir, natural)
    for h in range(2):

        def store(g, lanes, value):
            for c in range(CHUNKS):
                own, up, down = (
                    value[(r * CHUNKS + c) * rows : (r * CHUNKS + c + 1) * rows]
                    for r in range(3)
                )
                outs[c * 5][g, :, lanes] = own
                outs[c * 5 + 1 + h][g - h * half, :, lanes] = up
                outs[c * 5 + 3 + h][g - h * half, :, lanes] = down

        owner_order(natural, slot_block, (h * half, (h + 1) * half), store)


def partial_pieces(ao_blocks, blocks, occ_coeff, vir_coeff, owner, groups):
    slots, shell, _, width = ao_blocks.shape
    quarter, virtuals = vir_coeff.shape
    quarter_shells = quarter // shell
    steps = slots // SLOTS_PER_STEP
    inner = slots * shell
    rows = width // GRP // CHUNKS
    near_rows = 3 * CHUNKS * rows

    def vir_spec(k):
        return pl.BlockSpec(
            (shell, virtuals), lambda t, blk, own: (lax.rem(blk[k, 1], quarter_shells), 0)
        )

    vir_specs = [vir_spec(k) for k in range(slots)]
    full = jax.ShapeDtypeStruct((groups, rows, 256), BF)
    part = jax.ShapeDtypeStruct((groups // 2, rows, 256), BF)
    rest, *far = pl.pallas_call(
        functools.partial(
            far_kernel,
            slots=slots,
            groups=groups,
            width=width,
            shell=shell,
            quarter_shells=quarter_shells,
        ),
        grid_spec=pltpu.PrefetchScalarGridSpec(
            num_scalar_prefetch=2,
            grid=(steps,),
            in_specs=[
                pl.BlockSpec(occ_coeff.shape, lambda t, *_: (0, 0)),
                pl.BlockSpec((SLOTS_PER_STEP, shell, shell, width), lambda t, *_: (t, 0, 0, 0)),
            ]
            + vir_specs,
            out_specs=[VMEM] * (1 + 2 * CHUNKS),
            scratch_shapes=[
                pltpu.VMEM((2, inner, width), BF),
                pltpu.VMEM((width, 2 * inner), BF),
                pltpu.VMEM((CHUNKS * rows, 2 * inner), BF),
                pltpu.VMEM((virtuals // 64, CHUNKS * rows, 128), BF),
                pltpu.SMEM((owner.shape[0],), jnp.int32),
            ],
        ),
        out_shape=[jax.ShapeDtypeStruct((near_rows, 2 * inner), BF)] + [part] * (2 * CHUNKS),
        compiler_params=pltpu.CompilerParams(vmem_limit_bytes=52 * MIB),
        cost_estimate=pl.CostEstimate(
            flops=1024 * MIB, bytes_accessed=10 * MIB, transcendentals=0
        ),
        name="far_rows",
    )(blocks, owner, occ_coeff, ao_blocks, *([vir_coeff] * slots))
    near = pl.pallas_call(
        functools.partial(near_kernel, slots=slots, groups=groups),
        grid_spec=pltpu.PrefetchScalarGridSpec(
            num_scalar_prefetch=2,
            grid=(1,),
            in_specs=[VMEM] + vir_specs,
            out_specs=[VMEM] * (5 * CHUNKS),
            scratch_shapes=[
                pltpu.VMEM((virtuals // 64, near_rows, 128), BF),
                pltpu.SMEM((owner.shape[0],), jnp.int32),
            ],
        ),
        out_shape=([full] + [part] * 4) * CHUNKS,
        compiler_params=pltpu.CompilerParams(vmem_limit_bytes=32 * MIB),
        cost_estimate=pl.CostEstimate(
            flops=2 * 1024 * MIB, bytes_accessed=8 * MIB, transcendentals=0
        ),
        name="near_rows",
    )(blocks, owner, rest, *([vir_coeff] * slots))
    return far, near


def reorder_kernel(owner, x, *outs):
    rows = x.shape[1]
    blocks_per_occ = owner.shape[0] // 2
    lane = lax.broadcasted_iota(jnp.int32, (rows, 128), 1)
    for i in range(2):
        for t in range(blocks_per_occ // 2):
            tiles = []
            for j in range(2):
                d = owner[i * blocks_per_occ + t * 2 + j]
                lanes = pl.ds(pl.multiple_of(lax.rem(d // 2, 2) * 128, 128), 128)
                tiles.append(half_at(x[d // 4, :, lanes], d, j))
            outs[i][:, t * 128 : (t + 1) * 128] = jnp.where(lane < 64, tiles[0], tiles[1])


def reorder(x, owner):
    groups, rows, _ = x.shape
    return pl.pallas_call(
        reorder_kernel,
        in_specs=[SMEM, VMEM],
        out_specs=[VMEM, VMEM],
        out_shape=[jax.ShapeDtypeStruct((rows, groups * 128), BF)] * 2,
        compiler_params=pltpu.CompilerParams(vmem_limit_bytes=16 * MIB),
        cost_estimate=pl.CostEstimate(flops=0, bytes_accessed=2 * MIB, transcendentals=0),
        name="reorder_rows",
    )(owner, x)


def back_kernel(blocks, vir, *refs, quarter_shells, earlier_width):
    pieces = refs[: 2 * GRP]
    earlier = refs[2 * GRP] if earlier_width else None
    out, panel = refs[-2:]
    rows = pieces[0].shape[0]
    width = GRP * rows
    padded = panel.shape[0] // 2
    quarter = blocks[0, 1] // quarter_shells

    @pl.when(pl.program_id(0) == 0)
    def _():
        for i in range(2):
            for r in range(GRP):
                at = i * padded + lax.rem(quarter + r, GRP) * rows
                panel[pl.ds(pl.multiple_of(at, 16), rows), :] = pieces[r * 2 + i][...]
            if padded > width:
                panel[i * padded + width : (i + 1) * padded, :] = jnp.zeros(
                    (padded - width, panel.shape[1]), BF
                )

    both = lax.dot_general(
        vir[...], panel[...], (((1,), (1,)), ((), ())), preferred_element_type=F32
    ).astype(BF)
    for i in range(2):
        value = both[:, i * padded : i * padded + width]
        if earlier_width:
            value = jnp.concatenate([earlier[i], value], axis=1)
        out[i] = value


def back_transform(vir_coeff, blocks, shell, pieces, earlier=None):
    nus, virtuals = vir_coeff.shape
    rows = pieces[0].shape[0]
    width = GRP * rows
    padded = (width + 127) // 128 * 128
    earlier_width = 0 if earlier is None else earlier.shape[2]
    tile = 272
    more = () if earlier is None else (earlier,)
    return pl.pallas_call(
        functools.partial(
            back_kernel, quarter_shells=nus // shell, earlier_width=earlier_width
        ),
        grid=(nus // tile,),
        in_specs=[SMEM, pl.BlockSpec((tile, virtuals), lambda t: (t, 0))]
        + [VMEM] * (2 * GRP)
        + [pl.BlockSpec((2, tile, earlier_width), lambda t: (0, t, 0))] * len(more),
        out_specs=pl.BlockSpec((2, tile, width + earlier_width), lambda t: (0, t, 0)),
        out_shape=jax.ShapeDtypeStruct((2, nus, width + earlier_width), BF),
        scratch_shapes=[pltpu.VMEM((2 * padded, virtuals), BF)],
        compiler_params=pltpu.CompilerParams(vmem_limit_bytes=48 * MIB),
        cost_estimate=pl.CostEstimate(
            flops=2 * nus * virtuals * 2 * width, bytes_accessed=11 * MIB, transcendentals=0
        ),
        name="back_transform",
    )(blocks, vir_coeff, *pieces, *more)


def shift(value, by):
    return lax.ppermute(value, "grp", [(j, (j + by) % GRP) for j in range(GRP)])


def add(*terms):
    return sum(t.astype(F32) for t in terms).astype(BF)


def body(ao_blocks, blocks, occ_coeff, vir_coeff, occ_energy, vir_energy, owner):
    aux_place = lax.axis_index("aux")
    groups = lax.axis_size("aux")
    devices = groups * GRP
    virtuals = vir_coeff.shape[1]
    shell = ao_blocks.shape[1]
    block_rows = 2 * virtuals // devices
    half = groups // 2
    far, near = partial_pieces(ao_blocks, blocks, occ_coeff, vir_coeff, owner, groups)

    own_a, up_low_a, up_high_a, down_low_a, down_high_a = near[:5]
    own_b, up_low_b, up_high_b, down_low_b, down_high_b = near[5:]
    relay_up, relay_down = shift(far[0], 1), shift(far[1], -1)
    up_high_a, down_low_a = shift(up_high_a, 1), shift(down_low_a, -1)
    far_b = far[2:]
    *far_b, up_high_a, down_low_a = lax.optimization_barrier((*far_b, up_high_a, down_low_a))
    relay_up_b, relay_down_b = shift(far_b[0], 1), shift(far_b[1], -1)
    up_low_a = shift(add(up_low_a, relay_up), 1)
    down_high_a = shift(add(down_high_a, relay_down), -1)
    up_b = jnp.concatenate([add(up_low_b, relay_up_b), up_high_b], axis=0)
    down_b = jnp.concatenate([down_low_b, add(down_high_b, relay_down_b)], axis=0)
    up_b, down_b = shift(up_b, 1), shift(down_b, -1)
    totals = [
        jnp.concatenate(
            [add(own_a[:half], up_low_a, down_low_a), add(own_a[half:], up_high_a, down_high_a)],
            axis=0,
        ),
        add(own_b, up_b, down_b),
    ]
    arrived = []
    scores = None
    for total in totals:
        rows = lax.all_to_all(total, "aux", split_axis=0, concat_axis=0, tiled=True)
        rows = rows.reshape(-1, 4 * block_rows)
        arrived.append(rows)
        term = lax.dot_general(rows, rows, (((0,), (0,)), ((), ())), preferred_element_type=F32)
        scores = term if scores is None else scores + term

    members = aux_place * GRP + jnp.arange(GRP, dtype=jnp.int32)
    picked = owner[None, :] == members[:, None]
    pair_energy = (occ_energy[:, None] - vir_energy[None, :]).reshape(devices, block_rows)
    energy = jnp.sum(jnp.where(picked[:, :, None], pair_energy[None], 0.0), axis=1).reshape(-1)
    sent = scores.astype(BF)
    others = [shift(sent, by) for by in (1, 2, 3)]
    scores = scores + others[0].astype(F32) + others[1].astype(F32) + others[2].astype(F32)
    amplitude = (scores / (energy[:, None] + energy[None, :])).astype(BF)

    result = None
    for rows in arrived:
        density = jnp.dot(rows, amplitude, preferred_element_type=F32).astype(BF)
        density = density.reshape(groups, -1, 4 * block_rows)
        back = lax.all_to_all(density, "aux", split_axis=0, concat_axis=0, tiled=True)
        own = reorder(back, owner)
        below = [shift(own[0], 1), shift(own[1], 1)]
        above = [shift(own[0], -1), shift(own[1], -1)]
        distant = (shift(below[0], 1), shift(above[1], -1))
        result = back_transform(
            vir_coeff, blocks, shell, (*own, *above, *distant, *below), result
        )
    return result


def solution(mesh):
    return jax.shard_map(
        body,
        mesh=mesh,
        in_specs=(
            P(("aux", "grp"), None, None, None),
            P(("aux", "grp"), None),
            P(),
            P("grp", None),
            P(),
            P(),
            P(),
        ),
        out_specs=P(None, "grp", "aux"),
        check_vma=False,
    )
```

```python
import functools

import jax
import jax.numpy as jnp
from jax import lax
from jax.experimental import pallas as pl
from jax.experimental.pallas import tpu as pltpu
from jax.sharding import PartitionSpec as P

BF = jnp.bfloat16
F32 = jnp.float32
CHUNKS = 2
SLOTS_PER_STEP = 2
GRP = 4
MIB = 1024 * 1024
VMEM = pl.BlockSpec(memory_space=pltpu.VMEM)
SMEM = pl.BlockSpec(memory_space=pltpu.SMEM)


def swapped(tile):
    return jnp.concatenate([tile[:, 64:], tile[:, :64]], axis=1)


def half_at(tile, block, place):
    return jnp.where(lax.rem(block, 2) == place, tile, swapped(tile))


def invert(owner, slot_block):
    def put(b, carry):
        slot_block[owner[b]] = b
        return carry

    lax.fori_loop(0, owner.shape[0], put, 0)


def multiply(half_rows, vir, natural):
    inner = half_rows.shape[1] // 2
    tiles = natural.shape[0] // 2
    for t in range(tiles // 2):
        panel = jnp.concatenate([v[:, t * 256 : (t + 1) * 256] for v in vir], axis=0)
        for i in range(2):
            product = jnp.dot(
                half_rows[:, i * inner : (i + 1) * inner], panel, preferred_element_type=F32
            ).astype(BF)
            for j in range(2):
                natural[i * tiles + t * 2 + j] = product[:, j * 128 : (j + 1) * 128]


def owner_order(natural, slot_block, groups, store):
    lane = lax.broadcasted_iota(jnp.int32, natural.shape[1:], 1)

    def one(g):
        for pair in range(2):
            tiles = []
            for j in range(2):
                b = slot_block[g * 4 + pair * 2 + j]
                tiles.append(half_at(natural[b // 2], b, j))
            value = jnp.where(lane < 64, tiles[0], tiles[1])
            store(g, slice(pair * 128, (pair + 1) * 128), value)

    def two(t, carry):
        one(t * 2)
        one(t * 2 + 1)
        return carry

    lax.fori_loop(groups[0] // 2, groups[1] // 2, two, 0)


def far_kernel(blocks, owner, occ, ao, *refs, slots, groups, width, shell, quarter_shells):
    vir = refs[:slots]
    rest, *outs = refs[slots : slots + 1 + 2 * CHUNKS]
    half, half_abs, far_rows, natural, slot_block = refs[-5:]
    step = pl.program_id(0)
    inner = slots * shell
    rows = width // GRP // CHUNKS
    first_position = blocks[0, 2]
    quarter = blocks[0, 1] // quarter_shells

    position = lax.broadcasted_iota(jnp.int32, (shell, width), 1) + first_position
    spread = (128, shell * shell)
    source_lane = lax.broadcasted_iota(jnp.int32, spread, 0)
    target_mu = lax.broadcasted_iota(jnp.int32, spread, 1) // shell
    row = lax.broadcasted_iota(jnp.int32, (shell, shell * shell), 0)
    column = lax.broadcasted_iota(jnp.int32, (shell, shell * shell), 1)
    diagonal = lax.rem(column, shell) == row
    per_tile = 128 // shell
    for s in range(SLOTS_PER_STEP):
        k = step * SLOTS_PER_STEP + s
        inside = (position >= blocks[k, 2]) & (position < blocks[k, 3])
        mu_block = blocks[k, 0]
        lanes = pl.ds(pl.multiple_of((mu_block // per_tile) * 128, 128), 128)
        pick = source_lane == target_mu + lax.rem(mu_block, per_tile) * shell
        wide = jnp.dot(
            occ[:, lanes], jnp.where(pick, 1.0, 0.0).astype(BF), preferred_element_type=F32
        )
        weights = jnp.concatenate(
            [
                jnp.where(
                    diagonal, jnp.broadcast_to(wide[i : i + 1, :], (shell, shell * shell)), 0.0
                )
                for i in range(2)
            ],
            axis=0,
        ).astype(BF)
        both = jnp.dot(
            weights, ao[s].reshape(shell * shell, width), preferred_element_type=F32
        )
        for i in range(2):
            at = pl.ds(pl.multiple_of(k * shell, shell), shell)
            half[i, at, :] = jnp.where(inside, both[i * shell : (i + 1) * shell], 0.0).astype(BF)

    @pl.when(step == 0)
    def _():
        invert(owner, slot_block)

    @pl.when(step == slots // SLOTS_PER_STEP - 1)
    def _():
        for i in range(2):
            half_abs[:, i * inner : (i + 1) * inner] = half[i].T
        for at, r in enumerate((2, 0, 1, 3)):
            for c in range(CHUNKS):
                source = (c * GRP + lax.rem(quarter + r, GRP)) * rows
                value = half_abs[pl.ds(pl.multiple_of(source, 16), rows), :]
                if r == 2:
                    far_rows[c * rows : (c + 1) * rows, :] = value
                else:
                    begin = ((at - 1) * CHUNKS + c) * rows
                    rest[begin : begin + rows, :] = value
        multiply(far_rows, vir, natural)
        for h in range(2):

            def store(g, lanes, value):
                for c in range(CHUNKS):
                    outs[c * 2 + h][g - h * (groups // 2), :, lanes] = value[
                        c * rows : (c + 1) * rows
                    ]

            owner_order(
                natural, slot_block, (h * (groups // 2), (h + 1) * (groups // 2)), store
            )


def near_kernel(blocks, owner, half_rows, *refs, slots, groups):
    vir = refs[:slots]
    outs = refs[slots : slots + 5 * CHUNKS]
    natural, slot_block = refs[-2:]
    rows = half_rows.shape[0] // (3 * CHUNKS)
    half = groups // 2
    invert(owner, slot_block)
    multiply(half_rows, vir, natural)
    for h in range(2):

        def store(g, lanes, value):
            for c in range(CHUNKS):
                own, up, down = (
                    value[(r * CHUNKS + c) * rows : (r * CHUNKS + c + 1) * rows]
                    for r in range(3)
                )
                outs[c * 5][g, :, lanes] = own
                outs[c * 5 + 1 + h][g - h * half, :, lanes] = up
                outs[c * 5 + 3 + h][g - h * half, :, lanes] = down

        owner_order(natural, slot_block, (h * half, (h + 1) * half), store)


def partial_pieces(ao_blocks, blocks, occ_coeff, vir_coeff, owner, groups):
    slots, shell, _, width = ao_blocks.shape
    quarter, virtuals = vir_coeff.shape
    quarter_shells = quarter // shell
    steps = slots // SLOTS_PER_STEP
    inner = slots * shell
    rows = width // GRP // CHUNKS
    near_rows = 3 * CHUNKS * rows

    def vir_spec(k):
        return pl.BlockSpec(
            (shell, virtuals), lambda t, blk, own: (lax.rem(blk[k, 1], quarter_shells), 0)
        )

    vir_specs = [vir_spec(k) for k in range(slots)]
    full = jax.ShapeDtypeStruct((groups, rows, 256), BF)
    part = jax.ShapeDtypeStruct((groups // 2, rows, 256), BF)
    rest, *far = pl.pallas_call(
        functools.partial(
            far_kernel,
            slots=slots,
            groups=groups,
            width=width,
            shell=shell,
            quarter_shells=quarter_shells,
        ),
        grid_spec=pltpu.PrefetchScalarGridSpec(
            num_scalar_prefetch=2,
            grid=(steps,),
            in_specs=[
                pl.BlockSpec(occ_coeff.shape, lambda t, *_: (0, 0)),
                pl.BlockSpec((SLOTS_PER_STEP, shell, shell, width), lambda t, *_: (t, 0, 0, 0)),
            ]
            + vir_specs,
            out_specs=[VMEM] * (1 + 2 * CHUNKS),
            scratch_shapes=[
                pltpu.VMEM((2, inner, width), BF),
                pltpu.VMEM((width, 2 * inner), BF),
                pltpu.VMEM((CHUNKS * rows, 2 * inner), BF),
                pltpu.VMEM((virtuals // 64, CHUNKS * rows, 128), BF),
                pltpu.SMEM((owner.shape[0],), jnp.int32),
            ],
        ),
        out_shape=[jax.ShapeDtypeStruct((near_rows, 2 * inner), BF)] + [part] * (2 * CHUNKS),
        compiler_params=pltpu.CompilerParams(vmem_limit_bytes=52 * MIB),
        cost_estimate=pl.CostEstimate(
            flops=1024 * MIB, bytes_accessed=10 * MIB, transcendentals=0
        ),
        name="far_rows",
    )(blocks, owner, occ_coeff, ao_blocks, *([vir_coeff] * slots))
    near = pl.pallas_call(
        functools.partial(near_kernel, slots=slots, groups=groups),
        grid_spec=pltpu.PrefetchScalarGridSpec(
            num_scalar_prefetch=2,
            grid=(1,),
            in_specs=[VMEM] + vir_specs,
            out_specs=[VMEM] * (5 * CHUNKS),
            scratch_shapes=[
                pltpu.VMEM((virtuals // 64, near_rows, 128), BF),
                pltpu.SMEM((owner.shape[0],), jnp.int32),
            ],
        ),
        out_shape=([full] + [part] * 4) * CHUNKS,
        compiler_params=pltpu.CompilerParams(vmem_limit_bytes=32 * MIB),
        cost_estimate=pl.CostEstimate(
            flops=2 * 1024 * MIB, bytes_accessed=8 * MIB, transcendentals=0
        ),
        name="near_rows",
    )(blocks, owner, rest, *([vir_coeff] * slots))
    return far, near


def reorder_kernel(owner, x, *outs):
    rows = x.shape[1]
    blocks_per_occ = owner.shape[0] // 2
    lane = lax.broadcasted_iota(jnp.int32, (rows, 128), 1)
    for i in range(2):
        for t in range(blocks_per_occ // 2):
            tiles = []
            for j in range(2):
                d = owner[i * blocks_per_occ + t * 2 + j]
                lanes = pl.ds(pl.multiple_of(lax.rem(d // 2, 2) * 128, 128), 128)
                tiles.append(half_at(x[d // 4, :, lanes], d, j))
            outs[i][:, t * 128 : (t + 1) * 128] = jnp.where(lane < 64, tiles[0], tiles[1])


def reorder(x, owner):
    groups, rows, _ = x.shape
    return pl.pallas_call(
        reorder_kernel,
        in_specs=[SMEM, VMEM],
        out_specs=[VMEM, VMEM],
        out_shape=[jax.ShapeDtypeStruct((rows, groups * 128), BF)] * 2,
        compiler_params=pltpu.CompilerParams(vmem_limit_bytes=16 * MIB),
        cost_estimate=pl.CostEstimate(flops=0, bytes_accessed=2 * MIB, transcendentals=0),
        name="reorder_rows",
    )(owner, x)


def back_kernel(blocks, vir, *refs, quarter_shells, earlier_width):
    pieces = refs[: 2 * GRP]
    earlier = refs[2 * GRP] if earlier_width else None
    out, panel = refs[-2:]
    rows = pieces[0].shape[0]
    width = GRP * rows
    padded = panel.shape[0] // 2
    quarter = blocks[0, 1] // quarter_shells

    @pl.when(pl.program_id(0) == 0)
    def _():
        for i in range(2):
            for r in range(GRP):
                at = i * padded + lax.rem(quarter + r, GRP) * rows
                panel[pl.ds(pl.multiple_of(at, 16), rows), :] = pieces[r * 2 + i][...]
            if padded > width:
                panel[i * padded + width : (i + 1) * padded, :] = jnp.zeros(
                    (padded - width, panel.shape[1]), BF
                )

    both = lax.dot_general(
        vir[...], panel[...], (((1,), (1,)), ((), ())), preferred_element_type=F32
    ).astype(BF)
    for i in range(2):
        value = both[:, i * padded : i * padded + width]
        if earlier_width:
            value = jnp.concatenate([earlier[i], value], axis=1)
        out[i] = value


def back_transform(vir_coeff, blocks, shell, pieces, earlier=None):
    nus, virtuals = vir_coeff.shape
    rows = pieces[0].shape[0]
    width = GRP * rows
    padded = (width + 127) // 128 * 128
    earlier_width = 0 if earlier is None else earlier.shape[2]
    tile = 272
    more = () if earlier is None else (earlier,)
    return pl.pallas_call(
        functools.partial(
            back_kernel, quarter_shells=nus // shell, earlier_width=earlier_width
        ),
        grid=(nus // tile,),
        in_specs=[SMEM, pl.BlockSpec((tile, virtuals), lambda t: (t, 0))]
        + [VMEM] * (2 * GRP)
        + [pl.BlockSpec((2, tile, earlier_width), lambda t: (0, t, 0))] * len(more),
        out_specs=pl.BlockSpec((2, tile, width + earlier_width), lambda t: (0, t, 0)),
        out_shape=jax.ShapeDtypeStruct((2, nus, width + earlier_width), BF),
        scratch_shapes=[pltpu.VMEM((2 * padded, virtuals), BF)],
        compiler_params=pltpu.CompilerParams(vmem_limit_bytes=48 * MIB),
        cost_estimate=pl.CostEstimate(
            flops=2 * nus * virtuals * 2 * width, bytes_accessed=11 * MIB, transcendentals=0
        ),
        name="back_transform",
    )(blocks, vir_coeff, *pieces, *more)


def shift(value, by):
    return lax.ppermute(value, "grp", [(j, (j + by) % GRP) for j in range(GRP)])


def add(*terms):
    return sum(t.astype(F32) for t in terms).astype(BF)


def body(ao_blocks, blocks, occ_coeff, vir_coeff, occ_energy, vir_energy, owner):
    aux_place = lax.axis_index("aux")
    groups = lax.axis_size("aux")
    devices = groups * GRP
    virtuals = vir_coeff.shape[1]
    shell = ao_blocks.shape[1]
    block_rows = 2 * virtuals // devices
    half = groups // 2
    far, near = partial_pieces(ao_blocks, blocks, occ_coeff, vir_coeff, owner, groups)

    own_a, up_low_a, up_high_a, down_low_a, down_high_a = near[:5]
    own_b, up_low_b, up_high_b, down_low_b, down_high_b = near[5:]
    relay_up, relay_down = shift(far[0], 1), shift(far[1], -1)
    relay_up_b, relay_down_b = shift(far[2], 1), shift(far[3], -1)
    up_high_a, down_low_a, relay_up, relay_down = lax.optimization_barrier(
        (up_high_a, down_low_a, relay_up, relay_down)
    )
    up_high_a, down_low_a = shift(up_high_a, 1), shift(down_low_a, -1)
    up_low_a = shift(add(up_low_a, relay_up), 1)
    down_high_a = shift(add(down_high_a, relay_down), -1)
    up_b = jnp.concatenate([add(up_low_b, relay_up_b), up_high_b], axis=0)
    down_b = jnp.concatenate([down_low_b, add(down_high_b, relay_down_b)], axis=0)
    up_b, down_b, up_high_a, down_low_a = lax.optimization_barrier(
        (up_b, down_b, up_high_a, down_low_a)
    )
    up_b, down_b = shift(up_b, 1), shift(down_b, -1)
    totals = [
        jnp.concatenate(
            [add(own_a[:half], up_low_a, down_low_a), add(own_a[half:], up_high_a, down_high_a)],
            axis=0,
        ),
        add(own_b, up_b, down_b),
    ]
    arrived = []
    scores = None
    for total in totals:
        rows = lax.all_to_all(total, "aux", split_axis=0, concat_axis=0, tiled=True)
        rows = rows.reshape(-1, 4 * block_rows)
        arrived.append(rows)
        term = lax.dot_general(rows, rows, (((0,), (0,)), ((), ())), preferred_element_type=F32)
        scores = term if scores is None else scores + term

    members = aux_place * GRP + jnp.arange(GRP, dtype=jnp.int32)
    picked = owner[None, :] == members[:, None]
    pair_energy = (occ_energy[:, None] - vir_energy[None, :]).reshape(devices, block_rows)
    energy = jnp.sum(jnp.where(picked[:, :, None], pair_energy[None], 0.0), axis=1).reshape(-1)
    sent = scores.astype(BF)
    others = [shift(sent, by) for by in (1, 2, 3)]
    scores = scores + others[0].astype(F32) + others[1].astype(F32) + others[2].astype(F32)
    amplitude = (scores / (energy[:, None] + energy[None, :])).astype(BF)

    result = None
    for rows in arrived:
        density = jnp.dot(rows, amplitude, preferred_element_type=F32).astype(BF)
        density = density.reshape(groups, -1, 4 * block_rows)
        back = lax.all_to_all(density, "aux", split_axis=0, concat_axis=0, tiled=True)
        own = reorder(back, owner)
        below = [shift(own[0], 1), shift(own[1], 1)]
        above = [shift(own[0], -1), shift(own[1], -1)]
        distant = (shift(below[0], 1), shift(above[1], -1))
        result = back_transform(
            vir_coeff, blocks, shell, (*own, *above, *distant, *below), result
        )
    return result


def solution(mesh):
    return jax.shard_map(
        body,
        mesh=mesh,
        in_specs=(
            P(("aux", "grp"), None, None, None),
            P(("aux", "grp"), None),
            P(),
            P("grp", None),
            P(),
            P(),
            P(),
        ),
        out_specs=P(None, "grp", "aux"),
        check_vma=False,
    )
```

```python
import functools

import jax
import jax.numpy as jnp
from jax import lax
from jax.experimental import pallas as pl
from jax.experimental.pallas import tpu as pltpu
from jax.sharding import PartitionSpec as P

BF = jnp.bfloat16
F32 = jnp.float32
GRP = 4
MIB = 1024 * 1024
VMEM = pl.BlockSpec(memory_space=pltpu.VMEM)
ANY = pl.BlockSpec(memory_space=pl.ANY)
SMEM = pl.BlockSpec(memory_space=pltpu.SMEM)


def swapped(tile):
    return jnp.concatenate([tile[:, 64:], tile[:, :64]], axis=1)


def half_at(tile, block, place):
    return jnp.where(lax.rem(block, 2) == place, tile, swapped(tile))


def invert(owner, slot_block):
    def put(b, carry):
        slot_block[owner[b]] = b
        return carry

    lax.fori_loop(0, owner.shape[0], put, 0)


def multiply(half_rows, vir, natural):
    inner = half_rows.shape[1] // 2
    tiles = natural.shape[0] // 2
    for t in range(tiles // 2):
        panel = jnp.concatenate([v[:, t * 256 : (t + 1) * 256] for v in vir], axis=0)
        for i in range(2):
            product = jnp.dot(
                half_rows[:, i * inner : (i + 1) * inner], panel, preferred_element_type=F32
            ).astype(BF)
            for j in range(2):
                natural[i * tiles + t * 2 + j] = product[:, j * 128 : (j + 1) * 128]


def owner_order(natural, slot_block, groups, store):
    lane = lax.broadcasted_iota(jnp.int32, natural.shape[1:], 1)

    def one(g):
        for pair in range(2):
            tiles = []
            for j in range(2):
                b = slot_block[g * 4 + pair * 2 + j]
                tiles.append(half_at(natural[b // 2], b, j))
            value = jnp.where(lane < 64, tiles[0], tiles[1])
            store(g, slice(pair * 128, (pair + 1) * 128), value)

    def four(t, carry):
        for j in range(4):
            one(t * 4 + j)
        return carry

    lax.fori_loop(groups[0] // 4, groups[1] // 4, four, 0)


def far_kernel(blocks, owner, occ, ao, vir, rest, *refs, groups, quarter_shells):
    outs = refs[:4]
    tiles, vir_rows, half, half_abs, far_rows, natural, slot_block, arrived = refs[4:]
    slots, shell, _, width = ao.shape
    inner = slots * shell
    rows = width // GRP
    first_position = blocks[0, 2]
    quarter = blocks[0, 1] // quarter_shells

    copies = [pltpu.make_async_copy(ao.at[k], tiles.at[k], arrived.at[k]) for k in range(slots)]
    for k in range(slots):
        at = lax.rem(blocks[k, 1], quarter_shells) * shell
        copies.append(
            pltpu.make_async_copy(
                vir.at[pl.ds(pl.multiple_of(at, shell), shell), :],
                vir_rows.at[k],
                arrived.at[slots + k],
            )
        )
    for copy in copies:
        copy.start()
    invert(owner, slot_block)

    position = lax.broadcasted_iota(jnp.int32, (shell, width), 1) + first_position
    spread = (128, shell * shell)
    source_lane = lax.broadcasted_iota(jnp.int32, spread, 0)
    target_mu = lax.broadcasted_iota(jnp.int32, spread, 1) // shell
    row = lax.broadcasted_iota(jnp.int32, (shell, shell * shell), 0)
    column = lax.broadcasted_iota(jnp.int32, (shell, shell * shell), 1)
    diagonal = lax.rem(column, shell) == row
    per_tile = 128 // shell
    for k in range(slots):
        inside = (position >= blocks[k, 2]) & (position < blocks[k, 3])
        mu_block = blocks[k, 0]
        lanes = pl.ds(pl.multiple_of((mu_block // per_tile) * 128, 128), 128)
        pick = source_lane == target_mu + lax.rem(mu_block, per_tile) * shell
        wide = jnp.dot(
            occ[:, lanes], jnp.where(pick, 1.0, 0.0).astype(BF), preferred_element_type=F32
        )
        weights = jnp.concatenate(
            [
                jnp.where(
                    diagonal, jnp.broadcast_to(wide[i : i + 1, :], (shell, shell * shell)), 0.0
                )
                for i in range(2)
            ],
            axis=0,
        ).astype(BF)
        copies[k].wait()
        both = jnp.dot(
            weights, tiles[k].reshape(shell * shell, width), preferred_element_type=F32
        )
        for i in range(2):
            half[i, k * shell : (k + 1) * shell, :] = jnp.where(
                inside, both[i * shell : (i + 1) * shell], 0.0
            ).astype(BF)

    for i in range(2):
        half_abs[:, i * inner : (i + 1) * inner] = half[i].T
    for at, r in enumerate((2, 0, 1, 3)):
        source = lax.rem(quarter + r, GRP) * rows
        value = half_abs[pl.ds(pl.multiple_of(source, 32), rows), :]
        if r == 2:
            far_rows[...] = value
        else:
            rest[(at - 1) * rows : at * rows, :] = value
    for copy in copies[slots:]:
        copy.wait()
    multiply(far_rows, [vir_rows.at[k] for k in range(slots)], natural)
    part = groups // 4
    for p in range(4):

        def store(g, lanes, value):
            outs[p][g - p * part, :, lanes] = value

        owner_order(natural, slot_block, (p * part, (p + 1) * part), store)


def near_kernel(blocks, owner, half_rows, *refs, slots, groups):
    vir = refs[:slots]
    outs = refs[slots : slots + 10]
    natural, slot_block = refs[-2:]
    rows = half_rows.shape[0] // 3
    part = groups // 4
    invert(owner, slot_block)
    multiply(half_rows, vir, natural)
    for p in range(4):
        own, *sides = outs[p // 2 * 5 : p // 2 * 5 + 5]
        up, down = sides[p % 2], sides[2 + p % 2]

        def store(g, lanes, value):
            own[g - p // 2 * 2 * part, :, lanes] = value[:rows]
            up[g - p * part, :, lanes] = value[rows : 2 * rows]
            down[g - p * part, :, lanes] = value[2 * rows :]

        owner_order(natural, slot_block, (p * part, (p + 1) * part), store)


def partial_pieces(ao_blocks, blocks, occ_coeff, vir_coeff, owner, groups):
    slots, shell, _, width = ao_blocks.shape
    quarter, virtuals = vir_coeff.shape
    quarter_shells = quarter // shell
    inner = slots * shell
    rows = width // GRP
    near_rows = 3 * rows

    def vir_spec(k):
        return pl.BlockSpec(
            (shell, virtuals), lambda t, blk, own: (lax.rem(blk[k, 1], quarter_shells), 0)
        )

    vir_specs = [vir_spec(k) for k in range(slots)]
    full = jax.ShapeDtypeStruct((groups // 2, rows, 256), BF)
    part = jax.ShapeDtypeStruct((groups // 4, rows, 256), BF)
    rest, *far = pl.pallas_call(
        functools.partial(far_kernel, groups=groups, quarter_shells=quarter_shells),
        in_specs=[SMEM, SMEM, VMEM, ANY, ANY],
        out_specs=[VMEM] * 5,
        scratch_shapes=[
            pltpu.VMEM(ao_blocks.shape, BF),
            pltpu.VMEM((slots, shell, virtuals), BF),
            pltpu.VMEM((2, inner, width), BF),
            pltpu.VMEM((width, 2 * inner), BF),
            pltpu.VMEM((rows, 2 * inner), BF),
            pltpu.VMEM((virtuals // 64, rows, 128), BF),
            pltpu.SMEM((owner.shape[0],), jnp.int32),
            pltpu.SemaphoreType.DMA((2 * slots,)),
        ],
        out_shape=[jax.ShapeDtypeStruct((near_rows, 2 * inner), BF)] + [part] * 4,
        compiler_params=pltpu.CompilerParams(vmem_limit_bytes=52 * MIB),
        cost_estimate=pl.CostEstimate(
            flops=1024 * MIB, bytes_accessed=10 * MIB, transcendentals=0
        ),
        name="far_rows",
    )(blocks, owner, occ_coeff, ao_blocks, vir_coeff)
    near = pl.pallas_call(
        functools.partial(near_kernel, slots=slots, groups=groups),
        grid_spec=pltpu.PrefetchScalarGridSpec(
            num_scalar_prefetch=2,
            grid=(1,),
            in_specs=[VMEM] + vir_specs,
            out_specs=[VMEM] * 10,
            scratch_shapes=[
                pltpu.VMEM((virtuals // 64, near_rows, 128), BF),
                pltpu.SMEM((owner.shape[0],), jnp.int32),
            ],
        ),
        out_shape=([full] + [part] * 4) * 2,
        compiler_params=pltpu.CompilerParams(vmem_limit_bytes=32 * MIB),
        cost_estimate=pl.CostEstimate(
            flops=2 * 1024 * MIB, bytes_accessed=8 * MIB, transcendentals=0
        ),
        name="near_rows",
    )(blocks, owner, rest, *([vir_coeff] * slots))
    return far, near


def fill(owner, parts, raw, arrived, put):
    copies = []
    for r, given in enumerate(parts):
        begin = 0
        for k, part in enumerate(given):
            groups = part.shape[0]
            copies.append(
                pltpu.make_async_copy(
                    part, raw.at[r, begin : begin + groups], arrived.at[r * len(given) + k]
                )
            )
            begin += groups
    for copy in copies:
        copy.start()
    for copy in copies:
        copy.wait()
    blocks_per_occ = owner.shape[0] // 2
    lane = lax.broadcasted_iota(jnp.int32, (raw.shape[2], 128), 1)

    def one(i, t):
        found = [owner[i * blocks_per_occ + t * 2 + j] for j in range(2)]
        tiles = []
        for r in range(len(parts)):
            halves = []
            for j, d in enumerate(found):
                lanes = pl.ds(pl.multiple_of(lax.rem(d // 2, 2) * 128, 128), 128)
                halves.append(half_at(raw[r, d // 4, :, lanes], d, j))
            tiles.append(jnp.where(lane < 64, halves[0], halves[1]))
        put(i, pl.ds(pl.multiple_of(t * 128, 128), 128), tiles)

    def some(t, carry):
        for i in range(2):
            for k in range(4):
                one(i, t * 4 + k)
        return carry

    lax.fori_loop(0, blocks_per_occ // 8, some, 0)


def columns_kernel(blocks, owner, vir, *refs, quarter_shells, turns, more):
    out, raw, panel, arrived = refs[-4:]
    given = refs[: len(refs) - 4 - more]
    count = len(given) // len(turns)
    parts = [given[k * count : (k + 1) * count] for k in range(len(turns))]
    rows = raw.shape[2]
    width = len(turns) * rows
    quarter = blocks[0, 1] // quarter_shells

    @pl.when(pl.program_id(0) == 0)
    def _():
        def put(i, lanes, tiles):
            for k, tile in enumerate(tiles):
                begin = i * width + k * rows
                panel[begin : begin + rows, lanes] = tile

        fill(owner, parts, raw, arrived, put)

    both = lax.dot_general(
        vir[...], panel[...], (((1,), (1,)), ((), ())), preferred_element_type=F32
    ).astype(BF)
    source = lax.broadcasted_iota(jnp.int32, (width, out.shape[2]), 0)
    target = lax.broadcasted_iota(jnp.int32, (width, out.shape[2]), 1)
    pick = target < 0
    for k, r in enumerate(turns):
        moved = (lax.rem(quarter + r, GRP) - k) * rows
        pick = pick | ((source // rows == k) & (target == source + moved))
    pick = jnp.where(pick, 1.0, 0.0).astype(BF)
    for i in range(2):
        value = jnp.dot(
            both[:, i * width : (i + 1) * width], pick, preferred_element_type=F32
        )
        if more:
            value = value + refs[-5][i].astype(F32)
        out[i] = value.astype(BF)


def add_columns(vir, blocks, owner, shell, turns, pieces, earlier=None):
    nus, virtuals = vir.shape
    parts = [part for piece in pieces for part in piece]
    rows = parts[0].shape[1]
    groups = sum(part.shape[0] for part in pieces[0])
    tile = 272
    spec = pl.BlockSpec((2, tile, GRP * rows), lambda t: (0, t, 0))
    more = [] if earlier is None else [earlier]
    return pl.pallas_call(
        functools.partial(
            columns_kernel, quarter_shells=nus // shell, turns=turns, more=len(more)
        ),
        grid=(nus // tile,),
        in_specs=[SMEM, SMEM, pl.BlockSpec((tile, virtuals), lambda t: (t, 0))]
        + [VMEM] * len(parts)
        + [spec] * len(more),
        out_specs=spec,
        out_shape=jax.ShapeDtypeStruct((2, nus, GRP * rows), BF),
        scratch_shapes=[
            pltpu.VMEM((len(turns), groups, rows, 256), BF),
            pltpu.VMEM((2 * len(turns) * rows, virtuals), BF),
            pltpu.SemaphoreType.DMA((len(parts),)),
        ],
        compiler_params=pltpu.CompilerParams(vmem_limit_bytes=44 * MIB),
        cost_estimate=pl.CostEstimate(
            flops=4 * nus * virtuals * len(turns) * rows,
            bytes_accessed=12 * MIB,
            transcendentals=0,
        ),
        name="add_columns",
    )(blocks, owner, vir, *parts, *more)


def shift(value, by):
    return lax.ppermute(value, "grp", [(j, (j + by) % GRP) for j in range(GRP)])


def add(*terms):
    return sum(t.astype(F32) for t in terms).astype(BF)


def body(ao_blocks, blocks, occ_coeff, vir_coeff, occ_energy, vir_energy, owner):
    aux_place = lax.axis_index("aux")
    groups = lax.axis_size("aux")
    devices = groups * GRP
    virtuals = vir_coeff.shape[1]
    shell = ao_blocks.shape[1]
    block_rows = 2 * virtuals // devices
    quarter_groups = groups // 4
    far, near = partial_pieces(ao_blocks, blocks, occ_coeff, vir_coeff, owner, groups)

    own_a, up_low_a, up_high_a, down_low_a, down_high_a = near[:5]
    own_b, up_low_b, up_high_b, down_low_b, down_high_b = near[5:]
    relay_up, relay_down = shift(far[0], 1), shift(far[1], -1)
    relay_up_b, relay_down_b = shift(far[2], 1), shift(far[3], -1)
    up_high_a, down_low_a, relay_up, relay_down = lax.optimization_barrier(
        (up_high_a, down_low_a, relay_up, relay_down)
    )
    up_high_a, down_low_a = shift(up_high_a, 1), shift(down_low_a, -1)
    up_low_a = shift(add(up_low_a, relay_up), 1)
    down_high_a = shift(add(down_high_a, relay_down), -1)
    up_b = jnp.concatenate([add(up_low_b, relay_up_b), up_high_b], axis=0)
    down_b = jnp.concatenate([down_low_b, add(down_high_b, relay_down_b)], axis=0)
    up_b, down_b, up_high_a, down_low_a = lax.optimization_barrier(
        (up_b, down_b, up_high_a, down_low_a)
    )
    up_b, down_b = shift(up_b, 1), shift(down_b, -1)
    totals = [
        jnp.concatenate(
            [add(own_a[:quarter_groups], up_low_a, down_low_a),
                add(own_a[quarter_groups:], up_high_a, down_high_a),
            ],
            axis=0,
        ),
        add(own_b, up_b, down_b),
    ]
    def tie(values, *others):
        return list(lax.optimization_barrier((*values, *others)))[: len(values)]

    chips = groups // 2
    same_core = [[2 * j + core for j in range(chips)] for core in range(2)]

    def exchange(value):
        return lax.all_to_all(
            value, "aux", split_axis=0, concat_axis=0, axis_index_groups=same_core, tiled=True
        )

    pair_energy = (occ_energy[:, None] - vir_energy[None, :]).reshape(devices, block_rows)

    def amplitude_of(rows, h):
        members = (h * chips + aux_place // 2) * GRP + jnp.arange(GRP, dtype=jnp.int32)
        picked = owner[None, :] == members[:, None]
        energy = jnp.sum(jnp.where(picked[:, :, None], pair_energy[None], 0.0), axis=1).reshape(-1)
        scores = lax.dot_general(rows, rows, (((0,), (0,)), ((), ())), preferred_element_type=F32)
        scores = scores + lax.ppermute(scores, "aux", [(j, j ^ 1) for j in range(groups)])
        sent = scores.astype(BF)
        others = [shift(sent, by) for by in (1, 2, 3)]
        scores = scores + sum(other.astype(F32) for other in others)
        return (scores / (energy[:, None] + energy[None, :])).astype(BF)

    def density_of(rows, amplitude):
        density = jnp.dot(rows, amplitude, preferred_element_type=F32).astype(BF)
        return density.reshape(chips, -1, 4 * block_rows)

    def to_neighbours(own):
        parts = own[:quarter_groups], own[quarter_groups:]
        below = [shift(part, 1) for part in parts]
        above = [shift(part, -1) for part in parts]
        return parts, below, above

    rows_a = exchange(totals[0]).reshape(-1, 4 * block_rows)
    amplitude_a = amplitude_of(rows_a, 0)
    rows_b = exchange(totals[1]).reshape(-1, 4 * block_rows)
    rows_a, rows_b = tie((rows_a, rows_b))
    own_a, below_a, above_a = to_neighbours(exchange(density_of(rows_a, amplitude_a)))
    amplitude_b = amplitude_of(rows_b, 1)
    own_b, below_b, above_b = to_neighbours(exchange(density_of(rows_b, amplitude_b)))
    put = functools.partial(add_columns, vir_coeff, blocks, owner, shell)
    result = put((0,), [[*own_a, *own_b]])
    first, second, result = tie((below_a[0], above_a[1], result))
    far_a = [shift(first, 1), shift(second, -1)]
    far_b = [shift(below_b[0], 1), shift(above_b[1], -1)]
    result = put((1, 3), [[*above_a, *above_b], [*below_a, *below_b]], result)
    return put((2,), [[*far_a, *far_b]], result)


def solution(mesh):
    return jax.shard_map(
        body,
        mesh=mesh,
        in_specs=(
            P(("aux", "grp"), None, None, None),
            P(("aux", "grp"), None),
            P(),
            P("grp", None),
            P(),
            P(),
            P(),
        ),
        out_specs=P(None, "grp", "aux"),
        check_vma=False,
    )
```

```python
import functools

import jax
import jax.numpy as jnp
from jax import lax
from jax.experimental import pallas as pl
from jax.experimental.pallas import tpu as pltpu
from jax.sharding import PartitionSpec as P

BF = jnp.bfloat16
F32 = jnp.float32
GRP = 4
MIB = 1024 * 1024
VMEM = pl.BlockSpec(memory_space=pltpu.VMEM)
ANY = pl.BlockSpec(memory_space=pl.ANY)
SMEM = pl.BlockSpec(memory_space=pltpu.SMEM)


def swapped(tile):
    return jnp.concatenate([tile[:, 64:], tile[:, :64]], axis=1)


def half_at(tile, block, place):
    return jnp.where(lax.rem(block, 2) == place, tile, swapped(tile))


def invert(owner, slot_block):
    def put(b, carry):
        slot_block[owner[b]] = b
        return carry

    lax.fori_loop(0, owner.shape[0], put, 0)


def multiply(half_rows, vir, natural):
    inner = half_rows.shape[1] // 2
    tiles = natural.shape[0] // 2
    for t in range(tiles // 2):
        panel = jnp.concatenate([v[:, t * 256 : (t + 1) * 256] for v in vir], axis=0)
        for i in range(2):
            product = jnp.dot(
                half_rows[:, i * inner : (i + 1) * inner], panel, preferred_element_type=F32
            ).astype(BF)
            for j in range(2):
                natural[i * tiles + t * 2 + j] = product[:, j * 128 : (j + 1) * 128]


def owner_order(natural, slot_block, groups, store):
    lane = lax.broadcasted_iota(jnp.int32, natural.shape[1:], 1)

    def one(g):
        for pair in range(2):
            tiles = []
            for j in range(2):
                b = slot_block[g * 4 + pair * 2 + j]
                tiles.append(half_at(natural[b // 2], b, j))
            value = jnp.where(lane < 64, tiles[0], tiles[1])
            store(g, slice(pair * 128, (pair + 1) * 128), value)

    def four(t, carry):
        for j in range(4):
            one(t * 4 + j)
        return carry

    lax.fori_loop(groups[0] // 4, groups[1] // 4, four, 0)


def far_kernel(blocks, owner, occ, ao, vir, rest, *refs, groups, quarter_shells):
    outs = refs[:4]
    tiles, vir_rows, half, half_abs, far_rows, natural, slot_block, arrived = refs[4:]
    slots, shell, _, width = ao.shape
    inner = slots * shell
    rows = width // GRP
    first_position = blocks[0, 2]
    quarter = blocks[0, 1] // quarter_shells

    copies = [pltpu.make_async_copy(ao.at[k], tiles.at[k], arrived.at[k]) for k in range(slots)]
    for k in range(slots):
        at = lax.rem(blocks[k, 1], quarter_shells) * shell
        copies.append(
            pltpu.make_async_copy(
                vir.at[pl.ds(pl.multiple_of(at, shell), shell), :],
                vir_rows.at[k],
                arrived.at[slots + k],
            )
        )
    for copy in copies:
        copy.start()
    invert(owner, slot_block)

    position = lax.broadcasted_iota(jnp.int32, (shell, width), 1) + first_position
    spread = (128, shell * shell)
    source_lane = lax.broadcasted_iota(jnp.int32, spread, 0)
    target_mu = lax.broadcasted_iota(jnp.int32, spread, 1) // shell
    row = lax.broadcasted_iota(jnp.int32, (shell, shell * shell), 0)
    column = lax.broadcasted_iota(jnp.int32, (shell, shell * shell), 1)
    diagonal = lax.rem(column, shell) == row
    per_tile = 128 // shell
    for k in range(slots):
        inside = (position >= blocks[k, 2]) & (position < blocks[k, 3])
        mu_block = blocks[k, 0]
        lanes = pl.ds(pl.multiple_of((mu_block // per_tile) * 128, 128), 128)
        pick = source_lane == target_mu + lax.rem(mu_block, per_tile) * shell
        wide = jnp.dot(
            occ[:, lanes], jnp.where(pick, 1.0, 0.0).astype(BF), preferred_element_type=F32
        )
        weights = jnp.concatenate(
            [
                jnp.where(
                    diagonal, jnp.broadcast_to(wide[i : i + 1, :], (shell, shell * shell)), 0.0
                )
                for i in range(2)
            ],
            axis=0,
        ).astype(BF)
        copies[k].wait()
        both = jnp.dot(
            weights, tiles[k].reshape(shell * shell, width), preferred_element_type=F32
        )
        for i in range(2):
            half[i, k * shell : (k + 1) * shell, :] = jnp.where(
                inside, both[i * shell : (i + 1) * shell], 0.0
            ).astype(BF)

    for i in range(2):
        half_abs[:, i * inner : (i + 1) * inner] = half[i].T
    for at, r in enumerate((2, 0, 1, 3)):
        source = lax.rem(quarter + r, GRP) * rows
        value = half_abs[pl.ds(pl.multiple_of(source, 32), rows), :]
        if r == 2:
            far_rows[...] = value
        else:
            rest[(at - 1) * rows : at * rows, :] = value
    for copy in copies[slots:]:
        copy.wait()
    multiply(far_rows, [vir_rows.at[k] for k in range(slots)], natural)
    part = groups // 4
    for p in range(4):

        def store(g, lanes, value):
            outs[p][g - p * part, :, lanes] = value

        owner_order(natural, slot_block, (p * part, (p + 1) * part), store)


def near_kernel(blocks, owner, half_rows, *refs, slots, groups):
    vir = refs[:slots]
    outs = refs[slots : slots + 10]
    natural, slot_block = refs[-2:]
    rows = half_rows.shape[0] // 3
    part = groups // 4
    invert(owner, slot_block)
    multiply(half_rows, vir, natural)
    for p in range(4):
        own, *sides = outs[p // 2 * 5 : p // 2 * 5 + 5]
        up, down = sides[p % 2], sides[2 + p % 2]

        def store(g, lanes, value):
            own[g - p // 2 * 2 * part, :, lanes] = value[:rows]
            up[g - p * part, :, lanes] = value[rows : 2 * rows]
            down[g - p * part, :, lanes] = value[2 * rows :]

        owner_order(natural, slot_block, (p * part, (p + 1) * part), store)


def partial_pieces(ao_blocks, blocks, occ_coeff, vir_coeff, owner, groups):
    slots, shell, _, width = ao_blocks.shape
    quarter, virtuals = vir_coeff.shape
    quarter_shells = quarter // shell
    inner = slots * shell
    rows = width // GRP
    near_rows = 3 * rows

    def vir_spec(k):
        return pl.BlockSpec(
            (shell, virtuals), lambda t, blk, own: (lax.rem(blk[k, 1], quarter_shells), 0)
        )

    vir_specs = [vir_spec(k) for k in range(slots)]
    full = jax.ShapeDtypeStruct((groups // 2, rows, 256), BF)
    part = jax.ShapeDtypeStruct((groups // 4, rows, 256), BF)
    rest, *far = pl.pallas_call(
        functools.partial(far_kernel, groups=groups, quarter_shells=quarter_shells),
        in_specs=[SMEM, SMEM, VMEM, ANY, ANY],
        out_specs=[VMEM] * 5,
        scratch_shapes=[
            pltpu.VMEM(ao_blocks.shape, BF),
            pltpu.VMEM((slots, shell, virtuals), BF),
            pltpu.VMEM((2, inner, width), BF),
            pltpu.VMEM((width, 2 * inner), BF),
            pltpu.VMEM((rows, 2 * inner), BF),
            pltpu.VMEM((virtuals // 64, rows, 128), BF),
            pltpu.SMEM((owner.shape[0],), jnp.int32),
            pltpu.SemaphoreType.DMA((2 * slots,)),
        ],
        out_shape=[jax.ShapeDtypeStruct((near_rows, 2 * inner), BF)] + [part] * 4,
        compiler_params=pltpu.CompilerParams(vmem_limit_bytes=52 * MIB),
        cost_estimate=pl.CostEstimate(
            flops=1024 * MIB, bytes_accessed=10 * MIB, transcendentals=0
        ),
        name="far_rows",
    )(blocks, owner, occ_coeff, ao_blocks, vir_coeff)
    near = pl.pallas_call(
        functools.partial(near_kernel, slots=slots, groups=groups),
        grid_spec=pltpu.PrefetchScalarGridSpec(
            num_scalar_prefetch=2,
            grid=(1,),
            in_specs=[VMEM] + vir_specs,
            out_specs=[VMEM] * 10,
            scratch_shapes=[
                pltpu.VMEM((virtuals // 64, near_rows, 128), BF),
                pltpu.SMEM((owner.shape[0],), jnp.int32),
            ],
        ),
        out_shape=([full] + [part] * 4) * 2,
        compiler_params=pltpu.CompilerParams(vmem_limit_bytes=32 * MIB),
        cost_estimate=pl.CostEstimate(
            flops=2 * 1024 * MIB, bytes_accessed=8 * MIB, transcendentals=0
        ),
        name="near_rows",
    )(blocks, owner, rest, *([vir_coeff] * slots))
    return far, near


def fill(owner, raw, put):
    blocks_per_occ = owner.shape[0] // 2
    lane = lax.broadcasted_iota(jnp.int32, (raw.shape[2], 128), 1)

    def one(i, t):
        found = [owner[i * blocks_per_occ + t * 2 + j] for j in range(2)]
        tiles = []
        for r in range(raw.shape[0]):
            halves = []
            for j, d in enumerate(found):
                lanes = pl.ds(pl.multiple_of(lax.rem(d // 2, 2) * 128, 128), 128)
                halves.append(half_at(raw[r, d // 4, :, lanes], d, j))
            tiles.append(jnp.where(lane < 64, halves[0], halves[1]))
        put(i, pl.ds(pl.multiple_of(t * 128, 128), 128), tiles)

    def some(t, carry):
        for i in range(2):
            for k in range(4):
                one(i, t * 4 + k)
        return carry

    lax.fori_loop(0, blocks_per_occ // 8, some, 0)


def columns_kernel(blocks, owner, vir, *refs, quarter_shells, turns, more, last):
    out, raw, panel, held, arrived = refs[-5:]
    given = refs[: len(refs) - 5 - more]
    earlier = refs[-6] if more else None
    count = len(given) // len(turns)
    rows = raw.shape[2]
    width = len(turns) * rows
    quarter = blocks[0, 1] // quarter_shells
    strips = 2
    tile = vir.shape[0] // strips

    collect = []
    for at, part in enumerate(given):
        begin = (at % count) * part.shape[0]
        collect.append(
            pltpu.make_async_copy(
                part, raw.at[at // count, begin : begin + part.shape[0]], arrived.at[at]
            )
        )
    for copy in collect:
        copy.start()
    for copy in collect:
        copy.wait()

    def put(i, lanes, tiles):
        for k, value in enumerate(tiles):
            begin = i * width + k * rows
            panel[begin : begin + rows, lanes] = value

    fill(owner, raw, put)

    columns = GRP * rows
    source = lax.broadcasted_iota(jnp.int32, (width, columns), 0)
    target = lax.broadcasted_iota(jnp.int32, (width, columns), 1)
    pick = target < 0
    for k, r in enumerate(turns):
        moved = (lax.rem(quarter + r, GRP) - k) * rows
        pick = pick | ((source // rows == k) & (target == source + moved))
    pick = jnp.where(pick, 1.0, 0.0).astype(BF)
    stores = []
    for k in range(strips):
        here = slice(k * tile, (k + 1) * tile)
        both = lax.dot_general(
            vir[here, :], panel[...], (((1,), (1,)), ((), ())), preferred_element_type=F32
        ).astype(BF)
        for i in range(2):
            value = jnp.dot(
                both[:, i * width : (i + 1) * width], pick, preferred_element_type=F32
            )
            if more:
                value = value + earlier[i, here, :].astype(F32)
            if last:
                held[i, here, :] = value.astype(BF)
            else:
                out[i, here, :] = value.astype(BF)
        if last:
            stores.append(
                pltpu.make_async_copy(
                    held.at[:, here, :],
                    out.at[:, here, :],
                    arrived.at[len(given) + k],
                )
            )
            stores[-1].start()
    for copy in stores:
        copy.wait()


def add_columns(vir, blocks, owner, shell, turns, pieces, earlier=None, last=False):
    nus, virtuals = vir.shape
    parts = [part for piece in pieces for part in piece]
    rows = parts[0].shape[1]
    groups = sum(part.shape[0] for part in pieces[0])
    more = [] if earlier is None else [earlier]
    shape = (2, nus, GRP * rows)
    return pl.pallas_call(
        functools.partial(
            columns_kernel,
            quarter_shells=nus // shell,
            turns=turns,
            more=len(more),
            last=last,
        ),
        in_specs=[SMEM, SMEM] + [VMEM] * (1 + len(parts) + len(more)),
        out_specs=ANY if last else VMEM,
        out_shape=jax.ShapeDtypeStruct(shape, BF),
        scratch_shapes=[
            pltpu.VMEM((len(turns), groups, rows, 256), BF),
            pltpu.VMEM((2 * len(turns) * rows, virtuals), BF),
            pltpu.VMEM(shape if last else (2, 16, 128), BF),
            pltpu.SemaphoreType.DMA((len(parts) + 2,)),
        ],
        compiler_params=pltpu.CompilerParams(vmem_limit_bytes=24 * MIB),
        cost_estimate=pl.CostEstimate(
            flops=4 * nus * virtuals * len(turns) * rows,
            bytes_accessed=12 * MIB,
            transcendentals=0,
        ),
        name="add_columns",
    )(blocks, owner, vir, *parts, *more)


def shift(value, by):
    return lax.ppermute(value, "grp", [(j, (j + by) % GRP) for j in range(GRP)])


def add(*terms):
    return sum(t.astype(F32) for t in terms).astype(BF)


def body(ao_blocks, blocks, occ_coeff, vir_coeff, occ_energy, vir_energy, owner):
    aux_place = lax.axis_index("aux")
    groups = lax.axis_size("aux")
    devices = groups * GRP
    virtuals = vir_coeff.shape[1]
    shell = ao_blocks.shape[1]
    block_rows = 2 * virtuals // devices
    quarter_groups = groups // 4
    far, near = partial_pieces(ao_blocks, blocks, occ_coeff, vir_coeff, owner, groups)

    own_a, up_low_a, up_high_a, down_low_a, down_high_a = near[:5]
    own_b, up_low_b, up_high_b, down_low_b, down_high_b = near[5:]
    relay_up, relay_down = shift(far[0], 1), shift(far[1], -1)
    relay_up_b, relay_down_b = shift(far[2], 1), shift(far[3], -1)
    up_high_a, down_low_a, relay_up, relay_down = lax.optimization_barrier(
        (up_high_a, down_low_a, relay_up, relay_down)
    )
    up_high_a, down_low_a = shift(up_high_a, 1), shift(down_low_a, -1)
    up_low_a = shift(add(up_low_a, relay_up), 1)
    down_high_a = shift(add(down_high_a, relay_down), -1)
    up_b = jnp.concatenate([add(up_low_b, relay_up_b), up_high_b], axis=0)
    down_b = jnp.concatenate([down_low_b, add(down_high_b, relay_down_b)], axis=0)
    up_b, down_b, up_high_a, down_low_a = lax.optimization_barrier(
        (up_b, down_b, up_high_a, down_low_a)
    )
    up_b, down_b = shift(up_b, 1), shift(down_b, -1)
    totals = [
        jnp.concatenate(
            [add(own_a[:quarter_groups], up_low_a, down_low_a),
                add(own_a[quarter_groups:], up_high_a, down_high_a),
            ],
            axis=0,
        ),
        add(own_b, up_b, down_b),
    ]
    def tie(values, *others):
        return list(lax.optimization_barrier((*values, *others)))[: len(values)]

    chips = groups // 2
    same_core = [[2 * j + core for j in range(chips)] for core in range(2)]

    def exchange(value):
        return lax.all_to_all(
            value, "aux", split_axis=0, concat_axis=0, axis_index_groups=same_core, tiled=True
        )

    pair_energy = (occ_energy[:, None] - vir_energy[None, :]).reshape(devices, block_rows)

    def amplitude_of(rows, h):
        members = (h * chips + aux_place // 2) * GRP + jnp.arange(GRP, dtype=jnp.int32)
        picked = owner[None, :] == members[:, None]
        energy = jnp.sum(jnp.where(picked[:, :, None], pair_energy[None], 0.0), axis=1).reshape(-1)
        scores = lax.dot_general(rows, rows, (((0,), (0,)), ((), ())), preferred_element_type=F32)
        scores = scores + lax.ppermute(scores, "aux", [(j, j ^ 1) for j in range(groups)])
        sent = scores.astype(BF)
        others = [shift(sent, by) for by in (1, 2, 3)]
        scores = scores + sum(other.astype(F32) for other in others)
        return (scores / (energy[:, None] + energy[None, :])).astype(BF)

    def density_of(rows, amplitude):
        density = jnp.dot(rows, amplitude, preferred_element_type=F32).astype(BF)
        return density.reshape(chips, -1, 4 * block_rows)

    def to_neighbours(own):
        parts = own[:quarter_groups], own[quarter_groups:]
        below = [shift(part, 1) for part in parts]
        above = [shift(part, -1) for part in parts]
        return parts, below, above

    rows_a = exchange(totals[0]).reshape(-1, 4 * block_rows)
    amplitude_a = amplitude_of(rows_a, 0)
    rows_b = exchange(totals[1]).reshape(-1, 4 * block_rows)
    own_a, below_a, above_a = to_neighbours(exchange(density_of(rows_a, amplitude_a)))
    amplitude_b = amplitude_of(rows_b, 1)
    own_b, below_b, above_b = to_neighbours(exchange(density_of(rows_b, amplitude_b)))
    put = functools.partial(add_columns, vir_coeff, blocks, owner, shell)
    result = put((0,), [[*own_a, *own_b]])
    first, second, result = tie((below_a[0], above_a[1], result))
    far_a = [shift(first, 1), shift(second, -1)]
    far_b = [shift(below_b[0], 1), shift(above_b[1], -1)]
    result = put((1, 3), [[*above_a, *above_b], [*below_a, *below_b]], result)
    return put((2,), [[*far_a, *far_b]], result, last=True)


def solution(mesh):
    return jax.shard_map(
        body,
        mesh=mesh,
        in_specs=(
            P(("aux", "grp"), None, None, None),
            P(("aux", "grp"), None),
            P(),
            P("grp", None),
            P(),
            P(),
            P(),
        ),
        out_specs=P(None, "grp", "aux"),
        check_vma=False,
    )
```

```python
import functools

import jax
import jax.numpy as jnp
from jax import lax
from jax.experimental import pallas as pl
from jax.experimental.pallas import tpu as pltpu
from jax.sharding import PartitionSpec as P

BF = jnp.bfloat16
F32 = jnp.float32
GRP = 4
MIB = 1024 * 1024
VMEM = pl.BlockSpec(memory_space=pltpu.VMEM)
ANY = pl.BlockSpec(memory_space=pl.ANY)
SMEM = pl.BlockSpec(memory_space=pltpu.SMEM)


def swapped(tile):
    return jnp.concatenate([tile[:, 64:], tile[:, :64]], axis=1)


def half_at(tile, block, place):
    return jnp.where(lax.rem(block, 2) == place, tile, swapped(tile))


def invert(owner, slot_block):
    def put(b, carry):
        slot_block[owner[b]] = b
        return carry

    lax.fori_loop(0, owner.shape[0], put, 0)


def multiply(half_rows, vir, natural):
    inner = half_rows.shape[1] // 2
    tiles = natural.shape[0] // 2
    for t in range(tiles // 2):
        panel = jnp.concatenate([v[:, t * 256 : (t + 1) * 256] for v in vir], axis=0)
        for i in range(2):
            product = jnp.dot(
                half_rows[:, i * inner : (i + 1) * inner], panel, preferred_element_type=F32
            ).astype(BF)
            for j in range(2):
                natural[i * tiles + t * 2 + j] = product[:, j * 128 : (j + 1) * 128]


def owner_order(natural, slot_block, groups, store):
    lane = lax.broadcasted_iota(jnp.int32, natural.shape[1:], 1)

    def one(g):
        for pair in range(2):
            tiles = []
            for j in range(2):
                b = slot_block[g * 4 + pair * 2 + j]
                tiles.append(half_at(natural[b // 2], b, j))
            value = jnp.where(lane < 64, tiles[0], tiles[1])
            store(g, slice(pair * 128, (pair + 1) * 128), value)

    def four(t, carry):
        for j in range(4):
            one(t * 4 + j)
        return carry

    lax.fori_loop(groups[0] // 4, groups[1] // 4, four, 0)


def far_kernel(blocks, owner, occ, ao, vir, rest, *refs, groups, quarter_shells):
    outs = refs[:4]
    tiles, vir_rows, half, half_abs, far_rows, natural, slot_block, arrived = refs[4:]
    slots, shell, _, width = ao.shape
    inner = slots * shell
    rows = width // GRP
    first_position = blocks[0, 2]
    quarter = blocks[0, 1] // quarter_shells

    copies = [pltpu.make_async_copy(ao.at[k], tiles.at[k], arrived.at[k]) for k in range(slots)]
    for k in range(slots):
        at = lax.rem(blocks[k, 1], quarter_shells) * shell
        copies.append(
            pltpu.make_async_copy(
                vir.at[pl.ds(pl.multiple_of(at, shell), shell), :],
                vir_rows.at[k],
                arrived.at[slots + k],
            )
        )
    for copy in copies:
        copy.start()
    invert(owner, slot_block)

    position = lax.broadcasted_iota(jnp.int32, (shell, width), 1) + first_position
    spread = (128, shell * shell)
    source_lane = lax.broadcasted_iota(jnp.int32, spread, 0)
    target_mu = lax.broadcasted_iota(jnp.int32, spread, 1) // shell
    row = lax.broadcasted_iota(jnp.int32, (shell, shell * shell), 0)
    column = lax.broadcasted_iota(jnp.int32, (shell, shell * shell), 1)
    diagonal = lax.rem(column, shell) == row
    per_tile = 128 // shell
    for k in range(slots):
        inside = (position >= blocks[k, 2]) & (position < blocks[k, 3])
        mu_block = blocks[k, 0]
        lanes = pl.ds(pl.multiple_of((mu_block // per_tile) * 128, 128), 128)
        pick = source_lane == target_mu + lax.rem(mu_block, per_tile) * shell
        wide = jnp.dot(
            occ[:, lanes], jnp.where(pick, 1.0, 0.0).astype(BF), preferred_element_type=F32
        )
        weights = jnp.concatenate(
            [
                jnp.where(
                    diagonal, jnp.broadcast_to(wide[i : i + 1, :], (shell, shell * shell)), 0.0
                )
                for i in range(2)
            ],
            axis=0,
        ).astype(BF)
        copies[k].wait()
        both = jnp.dot(
            weights, tiles[k].reshape(shell * shell, width), preferred_element_type=F32
        )
        for i in range(2):
            half[i, k * shell : (k + 1) * shell, :] = jnp.where(
                inside, both[i * shell : (i + 1) * shell], 0.0
            ).astype(BF)

    for i in range(2):
        half_abs[:, i * inner : (i + 1) * inner] = half[i].T
    for at, r in enumerate((2, 0, 1, 3)):
        source = lax.rem(quarter + r, GRP) * rows
        value = half_abs[pl.ds(pl.multiple_of(source, 32), rows), :]
        if r == 2:
            far_rows[...] = value
        else:
            rest[(at - 1) * rows : at * rows, :] = value
    for copy in copies[slots:]:
        copy.wait()
    multiply(far_rows, [vir_rows.at[k] for k in range(slots)], natural)
    part = groups // 4
    for p in range(4):

        def store(g, lanes, value):
            outs[p][g - p * part, :, lanes] = value

        owner_order(natural, slot_block, (p * part, (p + 1) * part), store)


def near_kernel(blocks, owner, half_rows, *refs, slots, groups):
    vir = refs[:slots]
    outs = refs[slots : slots + 10]
    natural, slot_block = refs[-2:]
    rows = half_rows.shape[0] // 3
    part = groups // 4
    invert(owner, slot_block)
    multiply(half_rows, vir, natural)
    for p in range(4):
        own, *sides = outs[p // 2 * 5 : p // 2 * 5 + 5]
        up, down = sides[p % 2], sides[2 + p % 2]

        def store(g, lanes, value):
            own[g - p // 2 * 2 * part, :, lanes] = value[:rows]
            up[g - p * part, :, lanes] = value[rows : 2 * rows]
            down[g - p * part, :, lanes] = value[2 * rows :]

        owner_order(natural, slot_block, (p * part, (p + 1) * part), store)


def partial_pieces(ao_blocks, blocks, occ_coeff, vir_coeff, owner, groups):
    slots, shell, _, width = ao_blocks.shape
    quarter, virtuals = vir_coeff.shape
    quarter_shells = quarter // shell
    inner = slots * shell
    rows = width // GRP
    near_rows = 3 * rows

    def vir_spec(k):
        return pl.BlockSpec(
            (shell, virtuals), lambda t, blk, own: (lax.rem(blk[k, 1], quarter_shells), 0)
        )

    vir_specs = [vir_spec(k) for k in range(slots)]
    full = jax.ShapeDtypeStruct((groups // 2, rows, 256), BF)
    part = jax.ShapeDtypeStruct((groups // 4, rows, 256), BF)
    rest, *far = pl.pallas_call(
        functools.partial(far_kernel, groups=groups, quarter_shells=quarter_shells),
        in_specs=[SMEM, SMEM, VMEM, ANY, ANY],
        out_specs=[VMEM] * 5,
        scratch_shapes=[
            pltpu.VMEM(ao_blocks.shape, BF),
            pltpu.VMEM((slots, shell, virtuals), BF),
            pltpu.VMEM((2, inner, width), BF),
            pltpu.VMEM((width, 2 * inner), BF),
            pltpu.VMEM((rows, 2 * inner), BF),
            pltpu.VMEM((virtuals // 64, rows, 128), BF),
            pltpu.SMEM((owner.shape[0],), jnp.int32),
            pltpu.SemaphoreType.DMA((2 * slots,)),
        ],
        out_shape=[jax.ShapeDtypeStruct((near_rows, 2 * inner), BF)] + [part] * 4,
        compiler_params=pltpu.CompilerParams(vmem_limit_bytes=52 * MIB),
        cost_estimate=pl.CostEstimate(
            flops=1024 * MIB, bytes_accessed=10 * MIB, transcendentals=0
        ),
        name="far_rows",
    )(blocks, owner, occ_coeff, ao_blocks, vir_coeff)
    near = pl.pallas_call(
        functools.partial(near_kernel, slots=slots, groups=groups),
        grid_spec=pltpu.PrefetchScalarGridSpec(
            num_scalar_prefetch=2,
            grid=(1,),
            in_specs=[VMEM] + vir_specs,
            out_specs=[VMEM] * 10,
            scratch_shapes=[
                pltpu.VMEM((virtuals // 64, near_rows, 128), BF),
                pltpu.SMEM((owner.shape[0],), jnp.int32),
            ],
        ),
        out_shape=([full] + [part] * 4) * 2,
        compiler_params=pltpu.CompilerParams(vmem_limit_bytes=32 * MIB),
        cost_estimate=pl.CostEstimate(
            flops=2 * 1024 * MIB, bytes_accessed=8 * MIB, transcendentals=0
        ),
        name="near_rows",
    )(blocks, owner, rest, *([vir_coeff] * slots))
    return far, near


def fill(owner, raw, put):
    blocks_per_occ = owner.shape[0] // 2
    lane = lax.broadcasted_iota(jnp.int32, (raw.shape[2], 128), 1)

    def one(i, t):
        found = [owner[i * blocks_per_occ + t * 2 + j] for j in range(2)]
        tiles = []
        for r in range(raw.shape[0]):
            halves = []
            for j, d in enumerate(found):
                lanes = pl.ds(pl.multiple_of(lax.rem(d // 2, 2) * 128, 128), 128)
                halves.append(half_at(raw[r, d // 4, :, lanes], d, j))
            tiles.append(jnp.where(lane < 64, halves[0], halves[1]))
        put(i, pl.ds(pl.multiple_of(t * 128, 128), 128), tiles)

    def some(t, carry):
        for i in range(2):
            for k in range(4):
                one(i, t * 4 + k)
        return carry

    lax.fori_loop(0, blocks_per_occ // 8, some, 0)


def columns_kernel(blocks, owner, vir, *refs, quarter_shells, turns, more, last):
    out, raw, panel, held, arrived = refs[-5:]
    given = refs[: len(refs) - 5 - more]
    earlier = refs[-6] if more else None
    count = len(given) // len(turns)
    rows = raw.shape[2]
    width = len(turns) * rows
    quarter = blocks[0, 1] // quarter_shells
    target = held if last else out

    keep = []
    if more:
        keep = [pltpu.make_async_copy(earlier, target, arrived.at[len(given)])]
    collect = []
    for at, part in enumerate(given):
        begin = (at % count) * part.shape[0]
        collect.append(
            pltpu.make_async_copy(
                part, raw.at[at // count, begin : begin + part.shape[0]], arrived.at[at]
            )
        )
    for copy in collect + keep:
        copy.start()
    for copy in collect:
        copy.wait()

    def put(i, lanes, tiles):
        for k, value in enumerate(tiles):
            begin = i * width + k * rows
            panel[begin : begin + rows, lanes] = value

    fill(owner, raw, put)

    both = lax.dot_general(
        vir[...], panel[...], (((1,), (1,)), ((), ())), preferred_element_type=F32
    ).astype(BF)
    for copy in keep:
        copy.wait()
    for k, r in enumerate(turns):
        for q in range(GRP):

            @pl.when(lax.rem(quarter + r, GRP) == q)
            def _():
                for i in range(2):
                    begin = i * width + k * rows
                    target[i, :, q * rows : (q + 1) * rows] = both[:, begin : begin + rows]

    if last:
        store = pltpu.make_async_copy(held, out, arrived.at[len(given) + 1])
        store.start()
        store.wait()


def add_columns(vir, blocks, owner, shell, turns, pieces, earlier=None, last=False):
    nus, virtuals = vir.shape
    parts = [part for piece in pieces for part in piece]
    rows = parts[0].shape[1]
    groups = sum(part.shape[0] for part in pieces[0])
    more = [] if earlier is None else [earlier]
    shape = (2, nus, GRP * rows)
    return pl.pallas_call(
        functools.partial(
            columns_kernel,
            quarter_shells=nus // shell,
            turns=turns,
            more=len(more),
            last=last,
        ),
        in_specs=[SMEM, SMEM] + [VMEM] * (1 + len(parts) + len(more)),
        out_specs=ANY if last else VMEM,
        out_shape=jax.ShapeDtypeStruct(shape, BF),
        scratch_shapes=[
            pltpu.VMEM((len(turns), groups, rows, 256), BF),
            pltpu.VMEM((2 * len(turns) * rows, virtuals), BF),
            pltpu.VMEM(shape if last else (2, 16, 128), BF),
            pltpu.SemaphoreType.DMA((len(parts) + 2,)),
        ],
        compiler_params=pltpu.CompilerParams(vmem_limit_bytes=24 * MIB),
        cost_estimate=pl.CostEstimate(
            flops=4 * nus * virtuals * len(turns) * rows,
            bytes_accessed=12 * MIB,
            transcendentals=0,
        ),
        name="add_columns",
    )(blocks, owner, vir, *parts, *more)


def shift(value, by):
    return lax.ppermute(value, "grp", [(j, (j + by) % GRP) for j in range(GRP)])


def add(*terms):
    return sum(t.astype(F32) for t in terms).astype(BF)


def body(ao_blocks, blocks, occ_coeff, vir_coeff, occ_energy, vir_energy, owner):
    aux_place = lax.axis_index("aux")
    groups = lax.axis_size("aux")
    devices = groups * GRP
    virtuals = vir_coeff.shape[1]
    shell = ao_blocks.shape[1]
    block_rows = 2 * virtuals // devices
    quarter_groups = groups // 4
    far, near = partial_pieces(ao_blocks, blocks, occ_coeff, vir_coeff, owner, groups)

    own_a, up_low_a, up_high_a, down_low_a, down_high_a = near[:5]
    own_b, up_low_b, up_high_b, down_low_b, down_high_b = near[5:]
    relay_up, relay_down = shift(far[0], 1), shift(far[1], -1)
    relay_up_b, relay_down_b = shift(far[2], 1), shift(far[3], -1)
    up_high_a, down_low_a, relay_up, relay_down = lax.optimization_barrier(
        (up_high_a, down_low_a, relay_up, relay_down)
    )
    up_high_a, down_low_a = shift(up_high_a, 1), shift(down_low_a, -1)
    up_low_a = shift(add(up_low_a, relay_up), 1)
    down_high_a = shift(add(down_high_a, relay_down), -1)
    up_b = jnp.concatenate([add(up_low_b, relay_up_b), up_high_b], axis=0)
    down_b = jnp.concatenate([down_low_b, add(down_high_b, relay_down_b)], axis=0)
    up_b, down_b, up_high_a, down_low_a = lax.optimization_barrier(
        (up_b, down_b, up_high_a, down_low_a)
    )
    up_b, down_b = shift(up_b, 1), shift(down_b, -1)
    totals = [
        jnp.concatenate(
            [add(own_a[:quarter_groups], up_low_a, down_low_a),
                add(own_a[quarter_groups:], up_high_a, down_high_a),
            ],
            axis=0,
        ),
        add(own_b, up_b, down_b),
    ]
    def tie(values, *others):
        return list(lax.optimization_barrier((*values, *others)))[: len(values)]

    chips = groups // 2
    same_core = [[2 * j + core for j in range(chips)] for core in range(2)]

    def exchange(value):
        return lax.all_to_all(
            value, "aux", split_axis=0, concat_axis=0, axis_index_groups=same_core, tiled=True
        )

    pair_energy = (occ_energy[:, None] - vir_energy[None, :]).reshape(devices, block_rows)

    def amplitude_of(rows, h):
        members = (h * chips + aux_place // 2) * GRP + jnp.arange(GRP, dtype=jnp.int32)
        picked = owner[None, :] == members[:, None]
        energy = jnp.sum(jnp.where(picked[:, :, None], pair_energy[None], 0.0), axis=1).reshape(-1)
        scores = lax.dot_general(rows, rows, (((0,), (0,)), ((), ())), preferred_element_type=F32)
        scores = scores + lax.ppermute(scores, "aux", [(j, j ^ 1) for j in range(groups)])
        sent = scores.astype(BF)
        others = [shift(sent, by) for by in (1, 2, 3)]
        scores = scores + sum(other.astype(F32) for other in others)
        return (scores / (energy[:, None] + energy[None, :])).astype(BF)

    def density_of(rows, amplitude):
        density = jnp.dot(rows, amplitude, preferred_element_type=F32).astype(BF)
        return density.reshape(chips, -1, 4 * block_rows)

    def to_neighbours(own):
        parts = own[:quarter_groups], own[quarter_groups:]
        below = [shift(part, 1) for part in parts]
        above = [shift(part, -1) for part in parts]
        return parts, below, above

    rows_a = exchange(totals[0]).reshape(-1, 4 * block_rows)
    amplitude_a = amplitude_of(rows_a, 0)
    rows_b = exchange(totals[1]).reshape(-1, 4 * block_rows)
    own_a, below_a, above_a = to_neighbours(exchange(density_of(rows_a, amplitude_a)))
    amplitude_b = amplitude_of(rows_b, 1)
    own_b, below_b, above_b = to_neighbours(exchange(density_of(rows_b, amplitude_b)))
    put = functools.partial(add_columns, vir_coeff, blocks, owner, shell)
    result = put((0,), [[*own_a, *own_b]])
    first, second, result = tie((below_a[0], above_a[1], result))
    far_a = [shift(first, 1), shift(second, -1)]
    far_b = [shift(below_b[0], 1), shift(above_b[1], -1)]
    result = put((1, 3), [[*above_a, *above_b], [*below_a, *below_b]], result)
    return put((2,), [[*far_a, *far_b]], result, last=True)


def solution(mesh):
    return jax.shard_map(
        body,
        mesh=mesh,
        in_specs=(
            P(("aux", "grp"), None, None, None),
            P(("aux", "grp"), None),
            P(),
            P("grp", None),
            P(),
            P(),
            P(),
        ),
        out_specs=P(None, "grp", "aux"),
        check_vma=False,
    )
```

```python
import functools

import jax
import jax.numpy as jnp
from jax import lax
from jax.experimental import pallas as pl
from jax.experimental.pallas import tpu as pltpu
from jax.sharding import PartitionSpec as P

BF = jnp.bfloat16
F32 = jnp.float32
GRP = 4
MIB = 1024 * 1024
VMEM = pl.BlockSpec(memory_space=pltpu.VMEM)
ANY = pl.BlockSpec(memory_space=pl.ANY)
SMEM = pl.BlockSpec(memory_space=pltpu.SMEM)


def swapped(tile):
    return jnp.concatenate([tile[:, 64:], tile[:, :64]], axis=1)


def half_at(tile, block, place):
    return jnp.where(lax.rem(block, 2) == place, tile, swapped(tile))


def invert(owner, slot_block):
    def put(b, carry):
        slot_block[owner[b]] = b
        return carry

    lax.fori_loop(0, owner.shape[0], put, 0)


def multiply(half_rows, vir, natural):
    inner = half_rows.shape[1] // 2
    tiles = natural.shape[0] // 2
    for t in range(tiles // 2):
        panel = jnp.concatenate([v[:, t * 256 : (t + 1) * 256] for v in vir], axis=0)
        for i in range(2):
            product = jnp.dot(
                half_rows[:, i * inner : (i + 1) * inner], panel, preferred_element_type=F32
            ).astype(BF)
            for j in range(2):
                natural[i * tiles + t * 2 + j] = product[:, j * 128 : (j + 1) * 128]


def owner_order(natural, slot_block, groups, store):
    lane = lax.broadcasted_iota(jnp.int32, natural.shape[1:], 1)

    def one(g):
        for pair in range(2):
            tiles = []
            for j in range(2):
                b = slot_block[g * 4 + pair * 2 + j]
                tiles.append(half_at(natural[b // 2], b, j))
            value = jnp.where(lane < 64, tiles[0], tiles[1])
            store(g, slice(pair * 128, (pair + 1) * 128), value)

    def four(t, carry):
        for j in range(4):
            one(t * 4 + j)
        return carry

    lax.fori_loop(groups[0] // 4, groups[1] // 4, four, 0)


def far_kernel(blocks, owner, occ, ao, vir, rest, *refs, groups, quarter_shells):
    outs = refs[:4]
    tiles, vir_rows, half, half_abs, far_rows, natural, slot_block, arrived = refs[4:]
    slots, shell, _, width = ao.shape
    inner = slots * shell
    rows = width // GRP
    first_position = blocks[0, 2]
    quarter = blocks[0, 1] // quarter_shells

    copies = [pltpu.make_async_copy(ao.at[k], tiles.at[k], arrived.at[k]) for k in range(slots)]
    for k in range(slots):
        at = lax.rem(blocks[k, 1], quarter_shells) * shell
        copies.append(
            pltpu.make_async_copy(
                vir.at[pl.ds(pl.multiple_of(at, shell), shell), :],
                vir_rows.at[k],
                arrived.at[slots + k],
            )
        )
    for copy in copies:
        copy.start()
    invert(owner, slot_block)

    position = lax.broadcasted_iota(jnp.int32, (shell, width), 1) + first_position
    spread = (128, shell * shell)
    source_lane = lax.broadcasted_iota(jnp.int32, spread, 0)
    target_mu = lax.broadcasted_iota(jnp.int32, spread, 1) // shell
    row = lax.broadcasted_iota(jnp.int32, (shell, shell * shell), 0)
    column = lax.broadcasted_iota(jnp.int32, (shell, shell * shell), 1)
    diagonal = lax.rem(column, shell) == row
    per_tile = 128 // shell
    for k in range(slots):
        inside = (position >= blocks[k, 2]) & (position < blocks[k, 3])
        mu_block = blocks[k, 0]
        lanes = pl.ds(pl.multiple_of((mu_block // per_tile) * 128, 128), 128)
        pick = source_lane == target_mu + lax.rem(mu_block, per_tile) * shell
        wide = jnp.dot(
            occ[:, lanes], jnp.where(pick, 1.0, 0.0).astype(BF), preferred_element_type=F32
        )
        weights = jnp.concatenate(
            [
                jnp.where(
                    diagonal, jnp.broadcast_to(wide[i : i + 1, :], (shell, shell * shell)), 0.0
                )
                for i in range(2)
            ],
            axis=0,
        ).astype(BF)
        copies[k].wait()
        both = jnp.dot(
            weights, tiles[k].reshape(shell * shell, width), preferred_element_type=F32
        )
        for i in range(2):
            half[i, k * shell : (k + 1) * shell, :] = jnp.where(
                inside, both[i * shell : (i + 1) * shell], 0.0
            ).astype(BF)

    for i in range(2):
        half_abs[:, i * inner : (i + 1) * inner] = half[i].T
    for at, r in enumerate((2, 0, 1, 3)):
        source = lax.rem(quarter + r, GRP) * rows
        value = half_abs[pl.ds(pl.multiple_of(source, 32), rows), :]
        if r == 2:
            far_rows[...] = value
        else:
            rest[(at - 1) * rows : at * rows, :] = value
    for copy in copies[slots:]:
        copy.wait()
    multiply(far_rows, [vir_rows.at[k] for k in range(slots)], natural)
    part = groups // 4
    for p in range(4):

        def store(g, lanes, value):
            outs[p][g - p * part, :, lanes] = value

        owner_order(natural, slot_block, (p * part, (p + 1) * part), store)


def near_kernel(blocks, owner, half_rows, *refs, slots, groups):
    vir = refs[:slots]
    outs = refs[slots : slots + 10]
    natural, slot_block = refs[-2:]
    rows = half_rows.shape[0] // 3
    part = groups // 4
    invert(owner, slot_block)
    multiply(half_rows, vir, natural)
    for p in range(4):
        own, *sides = outs[p // 2 * 5 : p // 2 * 5 + 5]
        up, down = sides[p % 2], sides[2 + p % 2]

        def store(g, lanes, value):
            own[g - p // 2 * 2 * part, :, lanes] = value[:rows]
            up[g - p * part, :, lanes] = value[rows : 2 * rows]
            down[g - p * part, :, lanes] = value[2 * rows :]

        owner_order(natural, slot_block, (p * part, (p + 1) * part), store)


def partial_pieces(ao_blocks, blocks, occ_coeff, vir_coeff, owner, groups):
    slots, shell, _, width = ao_blocks.shape
    quarter, virtuals = vir_coeff.shape
    quarter_shells = quarter // shell
    inner = slots * shell
    rows = width // GRP
    near_rows = 3 * rows

    def vir_spec(k):
        return pl.BlockSpec(
            (shell, virtuals), lambda t, blk, own: (lax.rem(blk[k, 1], quarter_shells), 0)
        )

    vir_specs = [vir_spec(k) for k in range(slots)]
    full = jax.ShapeDtypeStruct((groups // 2, rows, 256), BF)
    part = jax.ShapeDtypeStruct((groups // 4, rows, 256), BF)
    rest, *far = pl.pallas_call(
        functools.partial(far_kernel, groups=groups, quarter_shells=quarter_shells),
        in_specs=[SMEM, SMEM, VMEM, ANY, ANY],
        out_specs=[VMEM] * 5,
        scratch_shapes=[
            pltpu.VMEM(ao_blocks.shape, BF),
            pltpu.VMEM((slots, shell, virtuals), BF),
            pltpu.VMEM((2, inner, width), BF),
            pltpu.VMEM((width, 2 * inner), BF),
            pltpu.VMEM((rows, 2 * inner), BF),
            pltpu.VMEM((virtuals // 64, rows, 128), BF),
            pltpu.SMEM((owner.shape[0],), jnp.int32),
            pltpu.SemaphoreType.DMA((2 * slots,)),
        ],
        out_shape=[jax.ShapeDtypeStruct((near_rows, 2 * inner), BF)] + [part] * 4,
        compiler_params=pltpu.CompilerParams(vmem_limit_bytes=52 * MIB),
        cost_estimate=pl.CostEstimate(
            flops=1024 * MIB, bytes_accessed=10 * MIB, transcendentals=0
        ),
        name="far_rows",
    )(blocks, owner, occ_coeff, ao_blocks, vir_coeff)
    near = pl.pallas_call(
        functools.partial(near_kernel, slots=slots, groups=groups),
        grid_spec=pltpu.PrefetchScalarGridSpec(
            num_scalar_prefetch=2,
            grid=(1,),
            in_specs=[VMEM] + vir_specs,
            out_specs=[VMEM] * 10,
            scratch_shapes=[
                pltpu.VMEM((virtuals // 64, near_rows, 128), BF),
                pltpu.SMEM((owner.shape[0],), jnp.int32),
            ],
        ),
        out_shape=([full] + [part] * 4) * 2,
        compiler_params=pltpu.CompilerParams(vmem_limit_bytes=32 * MIB),
        cost_estimate=pl.CostEstimate(
            flops=2 * 1024 * MIB, bytes_accessed=8 * MIB, transcendentals=0
        ),
        name="near_rows",
    )(blocks, owner, rest, *([vir_coeff] * slots))
    return far, near


def fill(owner, raw, put):
    blocks_per_occ = owner.shape[0] // 2
    lane = lax.broadcasted_iota(jnp.int32, (raw.shape[2], 128), 1)

    def one(i, t):
        found = [owner[i * blocks_per_occ + t * 2 + j] for j in range(2)]
        tiles = []
        for r in range(raw.shape[0]):
            halves = []
            for j, d in enumerate(found):
                lanes = pl.ds(pl.multiple_of(lax.rem(d // 2, 2) * 128, 128), 128)
                halves.append(half_at(raw[r, d // 4, :, lanes], d, j))
            tiles.append(jnp.where(lane < 64, halves[0], halves[1]))
        put(i, pl.ds(pl.multiple_of(t * 128, 128), 128), tiles)

    def some(t, carry):
        for i in range(2):
            for k in range(4):
                one(i, t * 4 + k)
        return carry

    lax.fori_loop(0, blocks_per_occ // 8, some, 0)


def columns_kernel(blocks, owner, vir, *refs, quarter_shells, turns, more, last):
    out, raw, panel, held, arrived = refs[-5:]
    given = refs[: len(refs) - 5 - more]
    earlier = refs[-6] if more else None
    count = len(given) // len(turns)
    rows = raw.shape[2]
    width = len(turns) * rows
    quarter = blocks[0, 1] // quarter_shells
    target = held if last else out

    keep = []
    if more:
        keep = [pltpu.make_async_copy(earlier, target, arrived.at[len(given)])]
    collect = []
    for at, part in enumerate(given):
        begin = (at % count) * part.shape[0]
        collect.append(
            pltpu.make_async_copy(
                part, raw.at[at // count, begin : begin + part.shape[0]], arrived.at[at]
            )
        )
    for copy in collect + keep:
        copy.start()
    for copy in collect:
        copy.wait()

    def put(i, lanes, tiles):
        for k, value in enumerate(tiles):
            begin = i * width + k * rows
            panel[begin : begin + rows, lanes] = value

    fill(owner, raw, put)

    both = lax.dot_general(
        vir[...], panel[...], (((1,), (1,)), ((), ())), preferred_element_type=F32
    ).astype(BF)
    for copy in keep:
        copy.wait()
    for k, r in enumerate(turns):
        for q in range(GRP):

            @pl.when(lax.rem(quarter + r, GRP) == q)
            def _():
                for i in range(2):
                    begin = i * width + k * rows
                    target[i, :, q * rows : (q + 1) * rows] = both[:, begin : begin + rows]

    if last:
        store = pltpu.make_async_copy(held, out, arrived.at[len(given) + 1])
        store.start()
        store.wait()


def add_columns(vir, blocks, owner, shell, turns, pieces, earlier=None, last=False):
    nus, virtuals = vir.shape
    parts = [part for piece in pieces for part in piece]
    rows = parts[0].shape[1]
    groups = sum(part.shape[0] for part in pieces[0])
    more = [] if earlier is None else [earlier]
    shape = (2, nus, GRP * rows)
    return pl.pallas_call(
        functools.partial(
            columns_kernel,
            quarter_shells=nus // shell,
            turns=turns,
            more=len(more),
            last=last,
        ),
        in_specs=[SMEM, SMEM] + [VMEM] * (1 + len(parts) + len(more)),
        out_specs=ANY if last else VMEM,
        out_shape=jax.ShapeDtypeStruct(shape, BF),
        scratch_shapes=[
            pltpu.VMEM((len(turns), groups, rows, 256), BF),
            pltpu.VMEM((2 * len(turns) * rows, virtuals), BF),
            pltpu.VMEM(shape if last else (2, 16, 128), BF),
            pltpu.SemaphoreType.DMA((len(parts) + 2,)),
        ],
        compiler_params=pltpu.CompilerParams(vmem_limit_bytes=24 * MIB),
        cost_estimate=pl.CostEstimate(
            flops=4 * nus * virtuals * len(turns) * rows,
            bytes_accessed=12 * MIB,
            transcendentals=0,
        ),
        name="add_columns",
    )(blocks, owner, vir, *parts, *more)


def shift(value, by):
    return lax.ppermute(value, "grp", [(j, (j + by) % GRP) for j in range(GRP)])


def add(*terms):
    return sum(t.astype(F32) for t in terms).astype(BF)


def body(ao_blocks, blocks, occ_coeff, vir_coeff, occ_energy, vir_energy, owner):
    aux_place = lax.axis_index("aux")
    groups = lax.axis_size("aux")
    devices = groups * GRP
    virtuals = vir_coeff.shape[1]
    shell = ao_blocks.shape[1]
    block_rows = 2 * virtuals // devices
    quarter_groups = groups // 4
    far, near = partial_pieces(ao_blocks, blocks, occ_coeff, vir_coeff, owner, groups)

    own_a, up_low_a, up_high_a, down_low_a, down_high_a = near[:5]
    own_b, up_low_b, up_high_b, down_low_b, down_high_b = near[5:]
    relay_up, relay_down = shift(far[0], 1), shift(far[1], -1)
    relay_up_b, relay_down_b = shift(far[2], 1), shift(far[3], -1)
    up_high_a, down_low_a, relay_up, relay_down = lax.optimization_barrier(
        (up_high_a, down_low_a, relay_up, relay_down)
    )
    up_high_a, down_low_a = shift(up_high_a, 1), shift(down_low_a, -1)
    up_low_a = shift(add(up_low_a, relay_up), 1)
    down_high_a = shift(add(down_high_a, relay_down), -1)
    up_b = jnp.concatenate([add(up_low_b, relay_up_b), up_high_b], axis=0)
    down_b = jnp.concatenate([down_low_b, add(down_high_b, relay_down_b)], axis=0)
    up_b, down_b, up_high_a, down_low_a = lax.optimization_barrier(
        (up_b, down_b, up_high_a, down_low_a)
    )
    up_b, down_b = shift(up_b, 1), shift(down_b, -1)
    totals = [
        jnp.concatenate(
            [add(own_a[:quarter_groups], up_low_a, down_low_a),
                add(own_a[quarter_groups:], up_high_a, down_high_a),
            ],
            axis=0,
        ),
        add(own_b, up_b, down_b),
    ]
    def tie(values, *others):
        return list(lax.optimization_barrier((*values, *others)))[: len(values)]

    chips = groups // 2
    same_core = [[2 * j + core for j in range(chips)] for core in range(2)]

    def exchange(value):
        return lax.all_to_all(
            value, "aux", split_axis=0, concat_axis=0, axis_index_groups=same_core, tiled=True
        )

    pair_energy = (occ_energy[:, None] - vir_energy[None, :]).reshape(devices, block_rows)

    def amplitude_of(rows, h):
        members = (h * chips + aux_place // 2) * GRP + jnp.arange(GRP, dtype=jnp.int32)
        picked = owner[None, :] == members[:, None]
        energy = jnp.sum(jnp.where(picked[:, :, None], pair_energy[None], 0.0), axis=1).reshape(-1)
        scores = lax.dot_general(rows, rows, (((0,), (0,)), ((), ())), preferred_element_type=F32)
        scores = scores + lax.ppermute(scores, "aux", [(j, j ^ 1) for j in range(groups)])
        sent = scores.astype(BF)
        others = [shift(sent, by) for by in (1, 2, 3)]
        scores = scores + sum(other.astype(F32) for other in others)
        return (scores / (energy[:, None] + energy[None, :])).astype(BF)

    def density_of(rows, amplitude):
        density = jnp.dot(rows, amplitude, preferred_element_type=F32).astype(BF)
        return density.reshape(chips, -1, 4 * block_rows)

    def to_neighbours(own):
        parts = own[:quarter_groups], own[quarter_groups:]
        below = [shift(part, 1) for part in parts]
        above = [shift(part, -1) for part in parts]
        return parts, below, above

    rows_a = exchange(totals[0]).reshape(-1, 4 * block_rows)
    amplitude_a = amplitude_of(rows_a, 0)
    rows_b = exchange(totals[1]).reshape(-1, 4 * block_rows)
    own_a, below_a, above_a = to_neighbours(exchange(density_of(rows_a, amplitude_a)))
    amplitude_b = amplitude_of(rows_b, 1)
    own_b, below_b, above_b = to_neighbours(exchange(density_of(rows_b, amplitude_b)))
    put = functools.partial(add_columns, vir_coeff, blocks, owner, shell)
    result = put((0,), [[*own_a, *own_b]])
    second, result = tie((above_a[1], result))
    far_a = [shift(below_a[0], 1), shift(second, -1)]
    far_b = [shift(below_b[0], 1), shift(above_b[1], -1)]
    result = put((1, 3), [[*above_a, *above_b], [*below_a, *below_b]], result)
    return put((2,), [[*far_a, *far_b]], result, last=True)


def solution(mesh):
    return jax.shard_map(
        body,
        mesh=mesh,
        in_specs=(
            P(("aux", "grp"), None, None, None),
            P(("aux", "grp"), None),
            P(),
            P("grp", None),
            P(),
            P(),
            P(),
        ),
        out_specs=P(None, "grp", "aux"),
        check_vma=False,
    )
```

```python
import functools

import jax
import jax.numpy as jnp
from jax import lax
from jax.experimental import pallas as pl
from jax.experimental.pallas import tpu as pltpu
from jax.sharding import PartitionSpec as P

BF = jnp.bfloat16
F32 = jnp.float32
GRP = 4
MIB = 1024 * 1024
VMEM = pl.BlockSpec(memory_space=pltpu.VMEM)
ANY = pl.BlockSpec(memory_space=pl.ANY)
SMEM = pl.BlockSpec(memory_space=pltpu.SMEM)


def swapped(tile):
    return jnp.concatenate([tile[:, 64:], tile[:, :64]], axis=1)


def half_at(tile, block, place):
    return jnp.where(lax.rem(block, 2) == place, tile, swapped(tile))


def invert(owner, slot_block):
    def put(b, carry):
        slot_block[owner[b]] = b
        return carry

    lax.fori_loop(0, owner.shape[0], put, 0)


def multiply(half_rows, vir, natural):
    inner = half_rows.shape[1] // 2
    tiles = natural.shape[0] // 2
    for t in range(tiles // 2):
        panel = jnp.concatenate([v[:, t * 256 : (t + 1) * 256] for v in vir], axis=0)
        for i in range(2):
            product = jnp.dot(
                half_rows[:, i * inner : (i + 1) * inner], panel, preferred_element_type=F32
            ).astype(BF)
            for j in range(2):
                natural[i * tiles + t * 2 + j] = product[:, j * 128 : (j + 1) * 128]


def owner_order(natural, slot_block, groups, store):
    lane = lax.broadcasted_iota(jnp.int32, natural.shape[1:], 1)

    def one(g):
        for pair in range(2):
            tiles = []
            for j in range(2):
                b = slot_block[g * 4 + pair * 2 + j]
                tiles.append(half_at(natural[b // 2], b, j))
            value = jnp.where(lane < 64, tiles[0], tiles[1])
            store(g, slice(pair * 128, (pair + 1) * 128), value)

    def four(t, carry):
        for j in range(4):
            one(t * 4 + j)
        return carry

    lax.fori_loop(groups[0] // 4, groups[1] // 4, four, 0)


def far_kernel(blocks, owner, occ, ao, vir, rest, *refs, groups, quarter_shells):
    outs = refs[:4]
    tiles, vir_rows, half, half_abs, far_rows, natural, slot_block, arrived = refs[4:]
    slots, shell, _, width = ao.shape
    inner = slots * shell
    rows = width // GRP
    first_position = blocks[0, 2]
    quarter = blocks[0, 1] // quarter_shells

    copies = [pltpu.make_async_copy(ao.at[k], tiles.at[k], arrived.at[k]) for k in range(slots)]
    for k in range(slots):
        at = lax.rem(blocks[k, 1], quarter_shells) * shell
        copies.append(
            pltpu.make_async_copy(
                vir.at[pl.ds(pl.multiple_of(at, shell), shell), :],
                vir_rows.at[k],
                arrived.at[slots + k],
            )
        )
    for copy in copies:
        copy.start()
    invert(owner, slot_block)

    position = lax.broadcasted_iota(jnp.int32, (shell, width), 1) + first_position
    spread = (128, shell * shell)
    source_lane = lax.broadcasted_iota(jnp.int32, spread, 0)
    target_mu = lax.broadcasted_iota(jnp.int32, spread, 1) // shell
    row = lax.broadcasted_iota(jnp.int32, (shell, shell * shell), 0)
    column = lax.broadcasted_iota(jnp.int32, (shell, shell * shell), 1)
    diagonal = lax.rem(column, shell) == row
    per_tile = 128 // shell
    for k in range(slots):
        inside = (position >= blocks[k, 2]) & (position < blocks[k, 3])
        mu_block = blocks[k, 0]
        lanes = pl.ds(pl.multiple_of((mu_block // per_tile) * 128, 128), 128)
        pick = source_lane == target_mu + lax.rem(mu_block, per_tile) * shell
        wide = jnp.dot(
            occ[:, lanes], jnp.where(pick, 1.0, 0.0).astype(BF), preferred_element_type=F32
        )
        weights = jnp.concatenate(
            [
                jnp.where(
                    diagonal, jnp.broadcast_to(wide[i : i + 1, :], (shell, shell * shell)), 0.0
                )
                for i in range(2)
            ],
            axis=0,
        ).astype(BF)
        copies[k].wait()
        both = jnp.dot(
            weights, tiles[k].reshape(shell * shell, width), preferred_element_type=F32
        )
        for i in range(2):
            half[i, k * shell : (k + 1) * shell, :] = jnp.where(
                inside, both[i * shell : (i + 1) * shell], 0.0
            ).astype(BF)

    for i in range(2):
        half_abs[:, i * inner : (i + 1) * inner] = half[i].T
    for at, r in enumerate((2, 0, 1, 3)):
        source = lax.rem(quarter + r, GRP) * rows
        value = half_abs[pl.ds(pl.multiple_of(source, 32), rows), :]
        if r == 2:
            far_rows[...] = value
        else:
            rest[(at - 1) * rows : at * rows, :] = value
    for copy in copies[slots:]:
        copy.wait()
    multiply(far_rows, [vir_rows.at[k] for k in range(slots)], natural)
    part = groups // 4
    for p in range(4):

        def store(g, lanes, value):
            outs[p][g - p * part, :, lanes] = value

        owner_order(natural, slot_block, (p * part, (p + 1) * part), store)


def near_kernel(blocks, owner, half_rows, *refs, slots, groups):
    vir = refs[:slots]
    outs = refs[slots : slots + 10]
    natural, slot_block = refs[-2:]
    rows = half_rows.shape[0] // 3
    part = groups // 4
    invert(owner, slot_block)
    multiply(half_rows, vir, natural)
    for p in range(4):
        own, *sides = outs[p // 2 * 5 : p // 2 * 5 + 5]
        up, down = sides[p % 2], sides[2 + p % 2]

        def store(g, lanes, value):
            own[g - p // 2 * 2 * part, :, lanes] = value[:rows]
            up[g - p * part, :, lanes] = value[rows : 2 * rows]
            down[g - p * part, :, lanes] = value[2 * rows :]

        owner_order(natural, slot_block, (p * part, (p + 1) * part), store)


def partial_pieces(ao_blocks, blocks, occ_coeff, vir_coeff, owner, groups):
    slots, shell, _, width = ao_blocks.shape
    quarter, virtuals = vir_coeff.shape
    quarter_shells = quarter // shell
    inner = slots * shell
    rows = width // GRP
    near_rows = 3 * rows

    def vir_spec(k):
        return pl.BlockSpec(
            (shell, virtuals), lambda t, blk, own: (lax.rem(blk[k, 1], quarter_shells), 0)
        )

    vir_specs = [vir_spec(k) for k in range(slots)]
    full = jax.ShapeDtypeStruct((groups // 2, rows, 256), BF)
    part = jax.ShapeDtypeStruct((groups // 4, rows, 256), BF)
    rest, *far = pl.pallas_call(
        functools.partial(far_kernel, groups=groups, quarter_shells=quarter_shells),
        in_specs=[SMEM, SMEM, VMEM, ANY, ANY],
        out_specs=[VMEM] * 5,
        scratch_shapes=[
            pltpu.VMEM(ao_blocks.shape, BF),
            pltpu.VMEM((slots, shell, virtuals), BF),
            pltpu.VMEM((2, inner, width), BF),
            pltpu.VMEM((width, 2 * inner), BF),
            pltpu.VMEM((rows, 2 * inner), BF),
            pltpu.VMEM((virtuals // 64, rows, 128), BF),
            pltpu.SMEM((owner.shape[0],), jnp.int32),
            pltpu.SemaphoreType.DMA((2 * slots,)),
        ],
        out_shape=[jax.ShapeDtypeStruct((near_rows, 2 * inner), BF)] + [part] * 4,
        compiler_params=pltpu.CompilerParams(vmem_limit_bytes=52 * MIB),
        cost_estimate=pl.CostEstimate(
            flops=1024 * MIB, bytes_accessed=10 * MIB, transcendentals=0
        ),
        name="far_rows",
    )(blocks, owner, occ_coeff, ao_blocks, vir_coeff)
    near = pl.pallas_call(
        functools.partial(near_kernel, slots=slots, groups=groups),
        grid_spec=pltpu.PrefetchScalarGridSpec(
            num_scalar_prefetch=2,
            grid=(1,),
            in_specs=[VMEM] + vir_specs,
            out_specs=[VMEM] * 10,
            scratch_shapes=[
                pltpu.VMEM((virtuals // 64, near_rows, 128), BF),
                pltpu.SMEM((owner.shape[0],), jnp.int32),
            ],
        ),
        out_shape=([full] + [part] * 4) * 2,
        compiler_params=pltpu.CompilerParams(vmem_limit_bytes=32 * MIB),
        cost_estimate=pl.CostEstimate(
            flops=2 * 1024 * MIB, bytes_accessed=8 * MIB, transcendentals=0
        ),
        name="near_rows",
    )(blocks, owner, rest, *([vir_coeff] * slots))
    return far, near


def fill(owner, raw, put):
    blocks_per_occ = owner.shape[0] // 2
    lane = lax.broadcasted_iota(jnp.int32, (raw.shape[2], 128), 1)

    def one(i, t):
        found = [owner[i * blocks_per_occ + t * 2 + j] for j in range(2)]
        tiles = []
        for r in range(raw.shape[0]):
            halves = []
            for j, d in enumerate(found):
                lanes = pl.ds(pl.multiple_of(lax.rem(d // 2, 2) * 128, 128), 128)
                halves.append(half_at(raw[r, d // 4, :, lanes], d, j))
            tiles.append(jnp.where(lane < 64, halves[0], halves[1]))
        put(i, pl.ds(pl.multiple_of(t * 128, 128), 128), tiles)

    def some(t, carry):
        for i in range(2):
            for k in range(4):
                one(i, t * 4 + k)
        return carry

    lax.fori_loop(0, blocks_per_occ // 8, some, 0)


def columns_kernel(blocks, owner, vir, *refs, quarter_shells, turns, more, last):
    out, raw, panel, held, arrived = refs[-5:]
    given = refs[: len(refs) - 5 - more]
    earlier = refs[-6] if more else None
    count = len(given) // len(turns)
    rows = raw.shape[2]
    width = len(turns) * rows
    quarter = blocks[0, 1] // quarter_shells
    target = held if last else out

    keep = []
    if more:
        keep = [pltpu.make_async_copy(earlier, target, arrived.at[len(given)])]
    collect = []
    for at, part in enumerate(given):
        begin = (at % count) * part.shape[0]
        collect.append(
            pltpu.make_async_copy(
                part, raw.at[at // count, begin : begin + part.shape[0]], arrived.at[at]
            )
        )
    for copy in collect + keep:
        copy.start()
    for copy in collect:
        copy.wait()

    def put(i, lanes, tiles):
        for k, value in enumerate(tiles):
            begin = i * width + k * rows
            panel[begin : begin + rows, lanes] = value

    fill(owner, raw, put)

    both = lax.dot_general(
        vir[...], panel[...], (((1,), (1,)), ((), ())), preferred_element_type=F32
    ).astype(BF)
    for copy in keep:
        copy.wait()
    stores = []
    for i in range(2):
        for k, r in enumerate(turns):
            for q in range(GRP):

                @pl.when(lax.rem(quarter + r, GRP) == q)
                def _():
                    begin = i * width + k * rows
                    target[i, :, q * rows : (q + 1) * rows] = both[:, begin : begin + rows]

        if last:
            stores.append(
                pltpu.make_async_copy(held.at[i], out.at[i], arrived.at[len(given) + 1 + i])
            )
            stores[-1].start()
    for store in stores:
        store.wait()


def add_columns(vir, blocks, owner, shell, turns, pieces, earlier=None, last=False):
    nus, virtuals = vir.shape
    parts = [part for piece in pieces for part in piece]
    rows = parts[0].shape[1]
    groups = sum(part.shape[0] for part in pieces[0])
    more = [] if earlier is None else [earlier]
    shape = (2, nus, GRP * rows)
    return pl.pallas_call(
        functools.partial(
            columns_kernel,
            quarter_shells=nus // shell,
            turns=turns,
            more=len(more),
            last=last,
        ),
        in_specs=[SMEM, SMEM] + [VMEM] * (1 + len(parts) + len(more)),
        out_specs=ANY if last else VMEM,
        out_shape=jax.ShapeDtypeStruct(shape, BF),
        scratch_shapes=[
            pltpu.VMEM((len(turns), groups, rows, 256), BF),
            pltpu.VMEM((2 * len(turns) * rows, virtuals), BF),
            pltpu.VMEM(shape if last else (2, 16, 128), BF),
            pltpu.SemaphoreType.DMA((len(parts) + 3,)),
        ],
        compiler_params=pltpu.CompilerParams(vmem_limit_bytes=24 * MIB),
        cost_estimate=pl.CostEstimate(
            flops=4 * nus * virtuals * len(turns) * rows,
            bytes_accessed=12 * MIB,
            transcendentals=0,
        ),
        name="add_columns",
    )(blocks, owner, vir, *parts, *more)


def shift(value, by):
    return lax.ppermute(value, "grp", [(j, (j + by) % GRP) for j in range(GRP)])


def add(*terms):
    return sum(t.astype(F32) for t in terms).astype(BF)


def body(ao_blocks, blocks, occ_coeff, vir_coeff, occ_energy, vir_energy, owner):
    aux_place = lax.axis_index("aux")
    groups = lax.axis_size("aux")
    devices = groups * GRP
    virtuals = vir_coeff.shape[1]
    shell = ao_blocks.shape[1]
    block_rows = 2 * virtuals // devices
    quarter_groups = groups // 4
    far, near = partial_pieces(ao_blocks, blocks, occ_coeff, vir_coeff, owner, groups)

    own_a, up_low_a, up_high_a, down_low_a, down_high_a = near[:5]
    own_b, up_low_b, up_high_b, down_low_b, down_high_b = near[5:]
    relay_up, relay_down = shift(far[0], 1), shift(far[1], -1)
    relay_up_b, relay_down_b = shift(far[2], 1), shift(far[3], -1)
    up_high_a, down_low_a, relay_up, relay_down = lax.optimization_barrier(
        (up_high_a, down_low_a, relay_up, relay_down)
    )
    up_high_a, down_low_a = shift(up_high_a, 1), shift(down_low_a, -1)
    up_low_a = shift(add(up_low_a, relay_up), 1)
    down_high_a = shift(add(down_high_a, relay_down), -1)
    up_b = jnp.concatenate([add(up_low_b, relay_up_b), up_high_b], axis=0)
    down_b = jnp.concatenate([down_low_b, add(down_high_b, relay_down_b)], axis=0)
    up_b, down_b, up_high_a, down_low_a = lax.optimization_barrier(
        (up_b, down_b, up_high_a, down_low_a)
    )
    up_b, down_b = shift(up_b, 1), shift(down_b, -1)
    totals = [
        jnp.concatenate(
            [add(own_a[:quarter_groups], up_low_a, down_low_a),
                add(own_a[quarter_groups:], up_high_a, down_high_a),
            ],
            axis=0,
        ),
        add(own_b, up_b, down_b),
    ]
    def tie(values, *others):
        return list(lax.optimization_barrier((*values, *others)))[: len(values)]

    chips = groups // 2
    same_core = [[2 * j + core for j in range(chips)] for core in range(2)]

    def exchange(value):
        return lax.all_to_all(
            value, "aux", split_axis=0, concat_axis=0, axis_index_groups=same_core, tiled=True
        )

    pair_energy = (occ_energy[:, None] - vir_energy[None, :]).reshape(devices, block_rows)

    def amplitude_of(rows, h):
        members = (h * chips + aux_place // 2) * GRP + jnp.arange(GRP, dtype=jnp.int32)
        picked = owner[None, :] == members[:, None]
        energy = jnp.sum(jnp.where(picked[:, :, None], pair_energy[None], 0.0), axis=1).reshape(-1)
        scores = lax.dot_general(rows, rows, (((0,), (0,)), ((), ())), preferred_element_type=F32)
        scores = scores + lax.ppermute(scores, "aux", [(j, j ^ 1) for j in range(groups)])
        sent = scores.astype(BF)
        others = [shift(sent, by) for by in (1, 2, 3)]
        scores = scores + sum(other.astype(F32) for other in others)
        return (scores / (energy[:, None] + energy[None, :])).astype(BF)

    def density_of(rows, amplitude):
        density = jnp.dot(rows, amplitude, preferred_element_type=F32).astype(BF)
        return density.reshape(chips, -1, 4 * block_rows)

    def to_neighbours(own):
        parts = own[:quarter_groups], own[quarter_groups:]
        below = [shift(part, 1) for part in parts]
        above = [shift(part, -1) for part in parts]
        return parts, below, above

    rows_a = exchange(totals[0]).reshape(-1, 4 * block_rows)
    amplitude_a = amplitude_of(rows_a, 0)
    rows_b = exchange(totals[1]).reshape(-1, 4 * block_rows)
    own_a, below_a, above_a = to_neighbours(exchange(density_of(rows_a, amplitude_a)))
    amplitude_b = amplitude_of(rows_b, 1)
    own_b, below_b, above_b = to_neighbours(exchange(density_of(rows_b, amplitude_b)))
    put = functools.partial(add_columns, vir_coeff, blocks, owner, shell)
    result = put((0,), [[*own_a, *own_b]])
    first, second, result = tie((below_a[0], above_a[1], result))
    far_a = [shift(first, 1), shift(second, -1)]
    far_b = [shift(below_b[0], 1), shift(above_b[1], -1)]
    result = put((1, 3), [[*above_a, *above_b], [*below_a, *below_b]], result)
    return put((2,), [[*far_a, *far_b]], result, last=True)


def solution(mesh):
    return jax.shard_map(
        body,
        mesh=mesh,
        in_specs=(
            P(("aux", "grp"), None, None, None),
            P(("aux", "grp"), None),
            P(),
            P("grp", None),
            P(),
            P(),
            P(),
        ),
        out_specs=P(None, "grp", "aux"),
        check_vma=False,
    )
```
